32 devices in a mesh: cfg: 2 (over y), tm: 8 (over z, x), space: 2 (over core).
Axes of the slice: x: 2, y: 2, z: 4, core: 2. Of those that a mesh axis runs over, the one named last changes fastest.
Arguments:
- vectors: bfloat16 [16, 2, 3, 8, 4, 16, 128], P(('cfg', 'tm'), None, None, 'space'), parts along dimension 0, may hold values from -6 to 6
- gauge_links: float32 [16, 3, 2, 3, 3, 8, 4, 16], P(('cfg', 'tm'), None, None, None, None, 'space'), parts along dimension 0, may hold values from -2.5 to 2.5
- perambulators: bfloat16 [16, 8, 4, 128, 256], P(('cfg', 'tm')), parts along dimension 0, may hold values from -0.375 to 0.375
- momenta: int32 [8, 3], replicated, may hold values from -2 to 2
- displacements: int32 [8], replicated, may hold values from 0 to 3, as said below
Outputs:
- elementals: bfloat16 [16, 8, 128, 256], P(('cfg', 'tm'), None, 'space'), parts along dimension 0
- correlators: float32 [8, 16, 8], P(None, ('cfg', 'tm')), parts along dimension 1
The draws below stay inside these ranges and needn't reach their ends.
There are 2 independent parts, one for each index of `cfg`. The reference program is written for one: setup_inputs(seed, part) draws one part's arguments, and reference() takes and returns one part's arrays. A program takes and returns all parts, laid end to end along the dimension named above; an argument that names none is the same for every part. Nothing has to cross between parts.
Inputs may be any that keep to these rules, and one draw needn't show every extreme that they name: `displacements`: each of the values 0, 1, 2, 3 appears exactly 2 times.
All inputs are finite; a program needn't handle non-finite values.
Results may differ from the reference program's by a relative error of at most 0.0075.
Values may be sent and summed in bfloat16 or wider, within the bound.
No kernel may reach another device: no remote copies, remote signals or barrier semaphores. Data moves between devices by JAX's collectives and lax.ppermute only.
A program may use at most 64 MiB of HBM per device.

```python
import math
import jax
import jax.numpy as jnp
from jax import lax

EIGEN_COUNT = 128
NSPIN = 4
NOP = 8
NDELTA = 8
LY = 4
LZ = 16
NT = 8
LX = 8
SITES = 512


def draw_displacements(key, part):
    pattern = jnp.arange(NOP, dtype=jnp.int32) % 4
    return jax.random.permutation(key, pattern)


def set_ends(entries, stream_key, low, largest):
    longest = entries.shape.index(max(entries.shape))
    spots = []
    for shift in (0, 1):
        where = [jax.random.randint(jax.random.fold_in(stream_key, axis), (), 0, length) for axis, length in enumerate(entries.shape)]
        where[longest] = (where[longest] + shift) % entries.shape[longest]
        spots.append(tuple(where))
    return entries.at[spots[0]].set(low).at[spots[1]].set(largest)


def levels(own_key, shape, shards, low, top_value):
    def one(axis_at, blocks):
        heights = jax.random.uniform(jax.random.fold_in(jax.random.fold_in(own_key, 6), axis_at), (blocks,), jnp.float32, low / len(shards), top_value / len(shards))
        return jnp.repeat(jnp.exp(heights), shape[axis_at] // blocks).reshape((-1,) + (1,) * (len(shape) - axis_at - 1))

    level = one(*shards[0])
    for cut in shards[1:]:
        level = level * one(*cut)
    return level


def gaussian(stream_key, shape, width, limit, cuts=(), held_as=jnp.bfloat16):
    result = jax.random.normal(stream_key, shape, jnp.float32) * width
    if len(cuts) > 0:
        result = levels(stream_key, shape, cuts, -0.22, 0.18) * result
    return jnp.clip(result, min=-limit, max=limit).astype(held_as)


def setup_inputs(seed: int = 0, part: int = 0) -> dict:
    arg_keys = jax.random.split(jax.random.key(seed), 6)
    part_keys = jax.random.split(jax.random.fold_in(arg_keys[5], part), 6)
    vectors = gaussian(part_keys[0], (NT, 2, 3, LX, LY, LZ, EIGEN_COUNT), 1.0, 6.0, ((0, 8), (3, 2)))
    gauge_links = gaussian(part_keys[1], (NT, 3, 2, 3, 3, LX, LY, LZ), 6 ** -0.5, 2.5, ((0, 8), (5, 2)), jnp.float32)
    perambulators = gaussian(part_keys[2], (NT, NDELTA, NSPIN, EIGEN_COUNT, 2 * EIGEN_COUNT), (2 * EIGEN_COUNT) ** -0.5, 0.375, ((0, 8),))
    momenta = set_ends(jax.random.randint(arg_keys[3], (NOP, 3), -2, 3), jax.random.fold_in(arg_keys[3], 1), -2, 2).astype(jnp.int32)
    displacements = draw_displacements(jax.random.fold_in(arg_keys[5], 71), part)
    return dict(vectors=vectors, gauge_links=gauge_links, perambulators=perambulators, momenta=momenta, displacements=displacements)


def link_times(link_matrix, vector_field):
    real_rows = []
    imag_rows = []
    for target in range(3):
        real_sum = jnp.zeros_like(vector_field[0, 0])
        imag_sum = jnp.zeros_like(vector_field[0, 0])
        for source in range(3):
            entry_real = link_matrix[0, target, source][..., None]
            entry_imag = link_matrix[1, target, source][..., None]
            real_sum = real_sum + entry_real * vector_field[0, source] - entry_imag * vector_field[1, source]
            imag_sum = imag_sum + entry_real * vector_field[1, source] + entry_imag * vector_field[0, source]
        real_rows.append(real_sum)
        imag_rows.append(imag_sum)
    return jnp.stack([jnp.stack(real_rows), jnp.stack(imag_rows)])

def adjoint(link_matrix):
    return jnp.stack([jnp.swapaxes(link_matrix[0], 0, 1), -jnp.swapaxes(link_matrix[1], 0, 1)])

def smeared_fields(vector_slice, link_slice):
    vector_field = vector_slice.astype(jnp.float32)
    neighbour_sum = jnp.zeros_like(vector_field)
    displaced = []
    for direction in range(3):
        spatial_axis = 2 + direction
        link_matrix = link_slice[direction]
        forward = link_times(link_matrix, jnp.roll(vector_field, -1, spatial_axis))
        backward = jnp.roll(link_times(adjoint(link_matrix), vector_field), 1, spatial_axis)
        neighbour_sum = neighbour_sum + forward + backward
        displaced.append(forward.astype(jnp.bfloat16))
    smoothed = (vector_field - neighbour_sum / 6.0).astype(jnp.bfloat16)
    return jnp.stack([smoothed] + displaced)

def phased(vector_slice, momentum, x_position, extent_x):
    extent_y = vector_slice.shape[3]
    extent_z = vector_slice.shape[4]
    y_position = jnp.arange(extent_y, dtype=jnp.int32).astype(jnp.float32)
    z_position = jnp.arange(extent_z, dtype=jnp.int32).astype(jnp.float32)
    momentum_float = momentum.astype(jnp.float32)
    phase_angle = (momentum_float[0] * x_position / extent_x)[:, None, None]
    phase_angle = phase_angle + (momentum_float[1] * y_position / extent_y)[None, :, None]
    phase_angle = phase_angle + (momentum_float[2] * z_position / extent_z)[None, None, :]
    phase_angle = 2.0 * math.pi * phase_angle
    cosine = jnp.cos(phase_angle)[..., None]
    sine_part = jnp.sin(phase_angle)[..., None]
    vector_field = vector_slice.astype(jnp.float32)
    left_real = vector_field[0] * cosine - vector_field[1] * sine_part
    left_imag = vector_field[0] * sine_part + vector_field[1] * cosine
    return jnp.stack([left_real, left_imag]).astype(jnp.bfloat16)

def project(left_field, right_field):
    column_entries = left_field.shape[-1]
    left_flat = left_field.reshape(-1, column_entries)
    rotated = jnp.stack([right_field[1], -right_field[0]])
    right_flat = jnp.concatenate([right_field.reshape(-1, column_entries), rotated.reshape(-1, column_entries)], axis=1)
    return jnp.dot(left_flat.T, right_flat, preferred_element_type=jnp.float32)

def operator_terms(fields, vector_slice, momenta, displacements, x_position, extent_x):
    partial_value = []
    for operator in range(momenta.shape[0]):
        left_field = phased(vector_slice, momenta[operator], x_position, extent_x)
        right_field = lax.dynamic_index_in_dim(fields, displacements[operator], 0, keepdims=False)
        partial_value.append(project(left_field, right_field))
    return jnp.stack(partial_value)

def sandwich_product(sink_elemental, peram_delta, row_start, row_count):
    column_entries = sink_elemental.shape[1]
    real_part = peram_delta[..., :column_entries]
    imag_part = peram_delta[..., column_entries:]
    block_matrix = jnp.concatenate([peram_delta, jnp.concatenate([-imag_part, real_part], axis=-1)], axis=1)
    flat_rows = sink_elemental.reshape(-1, 2 * column_entries)
    mixed_rows = jnp.einsum('mj,ajk->amk', flat_rows.astype(jnp.float32), block_matrix.astype(jnp.float32), precision=lax.Precision.HIGHEST).astype(jnp.bfloat16)
    mixed_rows = mixed_rows.reshape(peram_delta.shape[0], sink_elemental.shape[0], column_entries, 2 * column_entries)
    left_real = lax.dynamic_slice_in_dim(real_part, row_start, row_count, 2)
    left_imag = lax.dynamic_slice_in_dim(imag_part, row_start, row_count, 2)
    mixed_float = mixed_rows.astype(jnp.float32)
    first_factor = jnp.einsum('ail,aoik->olk', left_real.astype(jnp.float32), mixed_float, precision=lax.Precision.HIGHEST)
    second_factor = jnp.einsum('ail,aoik->olk', left_imag.astype(jnp.float32), mixed_float, precision=lax.Precision.HIGHEST)
    sandwich_real = first_factor[..., :column_entries] + second_factor[..., column_entries:]
    sandwich_imaginary = first_factor[..., column_entries:] - second_factor[..., :column_entries]
    return (sandwich_real, sandwich_imaginary)

def contract_meson(incoming_block, sandwich_real, sandwich_imaginary, eigen_total):
    column_entries = sandwich_real.shape[-1]
    incoming_block_float = incoming_block.astype(jnp.float32)
    grand_total = incoming_block_float[..., :column_entries] * sandwich_real + incoming_block_float[..., column_entries:] * sandwich_imaginary
    return lax.optimization_barrier(jnp.sum(grand_total, axis=(1, 2))) / eigen_total

def reference(vectors, gauge_links, perambulators, momenta, displacements):
    norm_factor = 1.0 / math.sqrt(6.0 * SITES)
    x_position = jnp.arange(LX, dtype=jnp.int32).astype(jnp.float32)

    def per_slice(packed):
        vector_slice, link_slice = packed
        fields = smeared_fields(vector_slice, link_slice)
        partial_value = operator_terms(fields, vector_slice, momenta, displacements, x_position, LX)
        return (partial_value * norm_factor).astype(jnp.bfloat16)
    elementals = lax.map(per_slice, (vectors, gauge_links))

    def per_sink(packed):
        slice_index, sink_elemental, perambulator_slice = packed
        earlier = (slice_index - jnp.arange(NDELTA, dtype=jnp.int32)) % NT
        source_times = jnp.take(elementals, earlier.astype(jnp.int32), axis=0)
        correlator_terms = []
        for time_separation in range(NDELTA):
            sandwich_real, sandwich_imaginary = sandwich_product(sink_elemental, perambulator_slice[time_separation], 0, EIGEN_COUNT)
            correlator_terms.append(contract_meson(source_times[time_separation], sandwich_real, sandwich_imaginary, EIGEN_COUNT))
        return jnp.stack(correlator_terms, axis=1)
    correlators = lax.map(per_sink, (jnp.arange(NT, dtype=jnp.int32), elementals, perambulators))
    return (elementals, jnp.transpose(correlators, (1, 0, 2)))
```

```python
import functools
import math

import jax
import jax.numpy as jnp
from jax import lax
from jax.experimental import pallas as pl
from jax.experimental.pallas import tpu as pltpu
from jax.sharding import PartitionSpec as P

ROWS = 16


def shift_pairs(count, steps):
    return [(i, (i + steps) % count) for i in range(count)]


def pick_operator(disp_ref, value, last):
    count = disp_ref.shape[0]
    first_seen = jnp.int32(count)
    last_seen = jnp.int32(-1)
    for o in range(count):
        hit = disp_ref[o] == value
        first_seen = jnp.where(hit, jnp.minimum(first_seen, o), first_seen)
        last_seen = jnp.where(hit, o, last_seen)
    return jnp.where(last == 0, first_seen, last_seen)


def link_product(entry, field, adjoint):
    real_rows, imag_rows = [], []
    for a in range(3):
        real_sum = imag_sum = None
        for b in range(3):
            if adjoint:
                u_real, u_imag = entry(0, b, a), entry(1, b, a)
                real_term = u_real * field[b] + u_imag * field[3 + b]
                imag_term = u_real * field[3 + b] - u_imag * field[b]
            else:
                u_real, u_imag = entry(0, a, b), entry(1, a, b)
                real_term = u_real * field[b] - u_imag * field[3 + b]
                imag_term = u_real * field[3 + b] + u_imag * field[b]
            real_sum = real_term if real_sum is None else real_sum + real_term
            imag_sum = imag_term if imag_sum is None else imag_sum + imag_term
        real_rows.append(real_sum)
        imag_rows.append(imag_sum)
    return real_rows + imag_rows


def elemental_kernel(
    wanted,
    norm_factor,
    disp_ref,
    mom_ref,
    own_ref,
    other_ref,
    own_links_ref,
    other_links_ref,
    phi_ref,
    vt_ref,
    links_ref,
    back_ref,
    left_ref,
    right_ref,
    turned_ref,
):
    half_x, ny, nz, eigen = own_ref.shape[1:]
    nx = 2 * half_x
    lanes = nx * nz
    side = lax.axis_index("space")
    lane = lax.broadcasted_iota(jnp.int32, (ROWS, lanes), 1)
    z_at = lane % nz
    smear = 0 in wanted

    def z_ahead(value):
        return jnp.where(
            z_at[: value.shape[0]] == nz - 1,
            pltpu.roll(value, nz - 1, 1),
            pltpu.roll(value, lanes - 1, 1),
        )

    def z_behind(value):
        return jnp.where(
            z_at[: value.shape[0]] == 0,
            pltpu.roll(value, lanes - (nz - 1), 1),
            pltpu.roll(value, 1, 1),
        )

    for y in range(ny):
        links_ref[y] = own_links_ref[y] + pltpu.roll(other_links_ref[y], lanes // 2, 1)
        if smear:
            for row in range(0, 18, 9):
                x_rows = links_ref[y, pl.ds(row, 9), :]
                back_ref[y, pl.ds(row, 9), :] = pltpu.roll(x_rows, nz, 1)
                z_rows = links_ref[y, pl.ds(36 + row, 9), :]
                back_ref[y, pl.ds(18 + row, 9), :] = z_behind(z_rows)
        for c in range(6):
            blocks = [own_ref[c, x, y] for x in range(half_x)]
            blocks += [other_ref[c, x, y] for x in range(half_x)]
            vt_ref[c, y] = jnp.concatenate(blocks, axis=0).astype(jnp.float32).T

    sub = lax.broadcasted_iota(jnp.int32, (8, lanes), 0)
    lane8 = lax.broadcasted_iota(jnp.int32, (8, lanes), 1)
    x_true = (lane8 // nz + half_x * side) % nx
    waves = []
    for value in wanted:
        o = pick_operator(disp_ref, value, side)
        turns = (
            mom_ref[o, 0] * x_true * (nz // nx)
            + mom_ref[o, 1] * sub * (nz // ny)
            + mom_ref[o, 2] * (lane8 % nz)
        )
        turns = ((turns + 8 * nz + nz // 2) % nz) - nz // 2
        angle = turns.astype(jnp.float32) * (2.0 * math.pi / nz)
        waves.append((jnp.cos(angle), jnp.sin(angle)))

    for y in range(ny):
        here = pl.ds(y * lanes, lanes)

        def chunk(e, carry, y=y, here=here):
            rows = pl.ds(pl.multiple_of(e * ROWS, ROWS), ROWS)
            lower = pl.ds(pl.multiple_of(e * ROWS + eigen, ROWS), ROWS)

            def entries(ref, base, y_at):
                return lambda part, a, b: ref[
                    y_at, pl.ds(base + part * 9 + a * 3 + b, 1), :
                ]

            def put(slot, values):
                for a in range(3):
                    real = values[a].astype(jnp.bfloat16)
                    imag = values[3 + a].astype(jnp.bfloat16)
                    right_ref[slot, a, rows, here] = real
                    right_ref[slot, a, lower, here] = imag
                    turned_ref[slot, a, rows, here] = imag
                    turned_ref[slot, a, lower, here] = -real

            field = [vt_ref[c, y, rows, :] for c in range(6)]
            for slot in range(len(wanted)):
                cosine = waves[slot][0][y : y + 1]
                sine = waves[slot][1][y : y + 1]
                for a in range(3):
                    real = field[a] * cosine - field[3 + a] * sine
                    imag = field[a] * sine + field[3 + a] * cosine
                    left_ref[slot, a, rows, here] = real.astype(jnp.bfloat16)
                    left_ref[slot, 3 + a, rows, here] = imag.astype(jnp.bfloat16)
            total = None
            for direction in (1, 2, 3):
                if not smear and direction not in wanted:
                    continue
                if direction == 1:
                    ahead = [pltpu.roll(f, lanes - nz, 1) for f in field]
                elif direction == 2:
                    ahead = [vt_ref[c, (y + 1) % ny, rows, :] for c in range(6)]
                else:
                    ahead = [z_ahead(f) for f in field]
                moved = link_product(
                    entries(links_ref, 18 * (direction - 1), y), ahead, False
                )
                if direction in wanted:
                    put(wanted.index(direction), moved)
                if smear:
                    total = moved if total is None else [p + q for p, q in zip(total, moved)]
                    if direction == 1:
                        behind = [pltpu.roll(f, nz, 1) for f in field]
                        entry = entries(back_ref, 0, y)
                    elif direction == 2:
                        behind = [vt_ref[c, (y - 1) % ny, rows, :] for c in range(6)]
                        entry = entries(links_ref, 18, (y - 1) % ny)
                    else:
                        behind = [z_behind(f) for f in field]
                        entry = entries(back_ref, 18, y)
                    moved = link_product(entry, behind, True)
                    total = [p + q for p, q in zip(total, moved)]
            if smear:
                put(wanted.index(0), [f - t * (1.0 / 6.0) for f, t in zip(field, total)])
            return carry

        lax.fori_loop(0, eigen // ROWS, chunk, 0)

    for slot in range(len(wanted)):
        total = None
        for a in range(3):
            for left, right in ((a, right_ref), (3 + a, turned_ref)):
                term = lax.dot_general(
                    left_ref[slot, left],
                    right[slot, a],
                    (((1,), (1,)), ((), ())),
                    preferred_element_type=jnp.float32,
                )
                total = term if total is None else total + term
        phi_ref[slot] = (total * norm_factor).astype(jnp.bfloat16)


def elementals(wanted, norm_factor, displacements, momenta, own, other, own_links, other_links):
    half_x, ny, nz, eigen = own.shape[1:]
    lanes = 2 * half_x * nz
    count = len(wanted)
    smem = pl.BlockSpec(memory_space=pltpu.SMEM)
    vmem = pl.BlockSpec(memory_space=pltpu.VMEM)
    sites = ny * lanes
    return pl.pallas_call(
        functools.partial(elemental_kernel, wanted, norm_factor),
        out_shape=jax.ShapeDtypeStruct((count, eigen, 2 * eigen), jnp.bfloat16),
        in_specs=[smem, smem, vmem, vmem, vmem, vmem],
        out_specs=vmem,
        scratch_shapes=[
            pltpu.VMEM((6, ny, eigen, lanes), jnp.float32),
            pltpu.VMEM((ny, 54, lanes), jnp.float32),
            pltpu.VMEM((ny, 36, lanes), jnp.float32),
            pltpu.VMEM((count, 6, eigen, sites), jnp.bfloat16),
            pltpu.VMEM((count, 3, 2 * eigen, sites), jnp.bfloat16),
            pltpu.VMEM((count, 3, 2 * eigen, sites), jnp.bfloat16),
        ],
        compiler_params=pltpu.CompilerParams(vmem_limit_bytes=32 * 1024 * 1024),
        cost_estimate=pl.CostEstimate(
            flops=count * 2 * 6 * sites * eigen * 2 * eigen,
            bytes_accessed=2 * own.size * 2,
            transcendentals=0,
        ),
        name="elementals_" + "".join(str(w) for w in wanted),
    )(displacements, momenta, own, other, own_links, other_links)


def sandwich_kernel(phi_ref, peram_ref, out_ref):
    count, eigen, _ = phi_ref.shape
    flat = phi_ref[...].reshape(count * eigen, 2 * eigen)
    totals = [None] * count
    for a in range(peram_ref.shape[1]):
        peram = peram_ref[0, a]
        real, imag = peram[:, :eigen], peram[:, eigen:]
        block = jnp.concatenate(
            [peram, jnp.concatenate([-imag, real], axis=1)], axis=0
        )
        mixed = jnp.dot(flat, block, preferred_element_type=jnp.float32)
        mixed = mixed.astype(jnp.bfloat16)
        adjoint = jnp.concatenate([real.T, imag.T], axis=1)
        for o in range(count):
            part = mixed[o * eigen : (o + 1) * eigen]
            turned = jnp.concatenate([part[:, eigen:], -part[:, :eigen]], axis=1)
            term = jnp.dot(
                adjoint,
                jnp.concatenate([part, turned], axis=0),
                preferred_element_type=jnp.float32,
            )
            totals[o] = term if totals[o] is None else totals[o] + term
    for o in range(count):
        out_ref[0, o] = totals[o]


def sandwiches(phi, perambulators):
    count, eigen, columns = phi.shape
    separations, spins = perambulators.shape[:2]
    return pl.pallas_call(
        sandwich_kernel,
        grid=(separations,),
        out_shape=jax.ShapeDtypeStruct((separations, count, eigen, columns), jnp.float32),
        in_specs=[
            pl.BlockSpec((count, eigen, columns), lambda d: (0, 0, 0)),
            pl.BlockSpec((1, spins, eigen, columns), lambda d: (d, 0, 0, 0)),
        ],
        out_specs=pl.BlockSpec((1, count, eigen, columns), lambda d: (d, 0, 0, 0)),
        compiler_params=pltpu.CompilerParams(vmem_limit_bytes=16 * 1024 * 1024),
        cost_estimate=pl.CostEstimate(
            flops=4 * separations * spins * count * eigen * columns * columns,
            bytes_accessed=2 * perambulators.size + 4 * separations * phi.size,
            transcendentals=0,
        ),
        name="sandwiches",
    )(phi, perambulators)


def contract_kernel(count, wanted, eigen_total, disp_ref, at_ref, *refs):
    table_ref, out_ref = refs[-2:]
    side = lax.axis_index("space")
    table = table_ref[...]
    row = lax.broadcasted_iota(jnp.int32, table.shape, 0)
    column = lax.broadcasted_iota(jnp.int32, table.shape, 1)
    for k in range(count):
        phi_ref, sand_ref = refs[2 * k], refs[2 * k + 1]
        for slot, value in enumerate(wanted[k]):
            o = pick_operator(disp_ref, value, side)
            product = phi_ref[slot].astype(jnp.float32) * sand_ref[0, slot]
            total = jnp.sum(product) * (1.0 / eigen_total)
            table = table + jnp.where((row == o) & (column == at_ref[k]), total, 0.0)
    out_ref[...] = table


def contract(displacements, at, arrivals, table):
    count = len(arrivals)
    operands, specs = [], []
    for k, (phi, sand, _) in enumerate(arrivals):
        operands += [phi, sand]
        specs.append(pl.BlockSpec(phi.shape, lambda i, disp, at: (0, 0, 0)))
        specs.append(
            pl.BlockSpec((1,) + sand.shape[1:], lambda i, disp, at, k=k: (at[k], 0, 0, 0))
        )
    whole = pl.BlockSpec(table.shape, lambda i, disp, at: (0, 0))
    eigen_total = arrivals[0][0].shape[1]
    return pl.pallas_call(
        functools.partial(
            contract_kernel, count, [wanted for _, _, wanted in arrivals], eigen_total
        ),
        grid_spec=pltpu.PrefetchScalarGridSpec(
            num_scalar_prefetch=2,
            grid=(1,),
            in_specs=specs + [whole],
            out_specs=whole,
        ),
        out_shape=jax.ShapeDtypeStruct(table.shape, jnp.float32),
        compiler_params=pltpu.CompilerParams(vmem_limit_bytes=16 * 1024 * 1024),
        cost_estimate=pl.CostEstimate(
            flops=2 * count * arrivals[0][0].size,
            bytes_accessed=6 * count * arrivals[0][0].size,
            transcendentals=0,
        ),
        name="contract",
    )(displacements, at, *operands, table)


def spread(groups, separations):
    count = lax.axis_size("tm")
    me = lax.axis_index("tm")
    arrivals = [[(g, jnp.int32(0))] for g in groups]
    if count == separations:
        order = list(range(0, count, 2)) + list(range(count - 1, 0, -2))
        place = jnp.zeros((), jnp.int32)
        for k, t in enumerate(order):
            place = jnp.where(me == t, k, place)
        ahead = [(order[k], order[(k + 1) % count]) for k in range(count)]
        behind = [(b, a) for a, b in ahead]

        def owner(steps):
            at = (place - steps) % count
            t = jnp.zeros((), jnp.int32)
            for k, slice_index in enumerate(order):
                t = jnp.where(at == k, slice_index, t)
            return (me - t) % count

        for index, group in enumerate(groups):
            forward = backward = group
            many = count // 2 if index % 2 == 0 else (count - 1) // 2
            few = count - 1 - many
            for step in range(1, count // 2 + 1):
                if step <= many:
                    forward = lax.ppermute(forward, "tm", ahead)
                    arrivals[index].append((forward, owner(step)))
                if step <= few:
                    backward = lax.ppermute(backward, "tm", behind)
                    arrivals[index].append((backward, owner(-step)))
    else:
        for index, group in enumerate(groups):
            for step in range(1, separations):
                group = lax.ppermute(group, "tm", shift_pairs(count, 1))
                arrivals[index].append((group, jnp.int32(step)))
    return arrivals


def body(vectors, gauge_links, perambulators, momenta, displacements):
    side = lax.axis_index("space")
    swap = [(0, 1), (1, 0)]
    half_x, ny, nz, eigen = vectors.shape[3:]
    own = vectors.reshape((6, half_x, ny, nz, eigen))
    other = lax.ppermute(own, "space", swap)
    own_links = gauge_links.reshape((54, half_x, ny, nz)).transpose((2, 0, 1, 3))
    own_links = own_links.reshape((ny, 54, half_x * nz))
    own_links = jnp.pad(own_links, ((0, 0), (0, 0), (0, half_x * nz)))
    other_links = lax.ppermute(own_links, "space", swap)
    norm_factor = 1.0 / math.sqrt(6.0 * 2 * half_x * ny * nz)
    groups = ((2, 3), (1, 0))
    phis = [
        elementals(
            wanted, norm_factor, displacements, momenta, own, other, own_links, other_links
        )
        for wanted in groups
    ]
    separations = perambulators.shape[1]
    arrivals = spread(phis, separations)
    sands = [sandwiches(phi, perambulators[0]) for phi in phis]
    table = jnp.zeros((momenta.shape[0], separations), jnp.float32)
    for step in range(0, separations, 2):
        batch, at = [], []
        for index in range(len(groups)):
            for rows, separation in arrivals[index][step : step + 2]:
                batch.append((rows, sands[index], groups[index]))
                at.append(separation)
        table = contract(displacements, jnp.stack(at).astype(jnp.int32), batch, table)
    correlators = table + lax.ppermute(table, "space", swap)

    half_rows = eigen // 2
    mine = jnp.concatenate(phis, axis=0)
    kept = lax.dynamic_slice_in_dim(mine, side * half_rows, half_rows, 1)
    given = lax.dynamic_slice_in_dim(mine, (1 - side) * half_rows, half_rows, 1)
    taken = lax.ppermute(given, "space", swap)
    both = jnp.concatenate([kept, taken], axis=0)
    values = jnp.array([v for wanted in groups for v in wanted], jnp.int32)
    slot = jnp.argmax(displacements[:, None] == values[None, :], axis=1).astype(jnp.int32)
    seen = jnp.sum(
        (displacements[:, None] == displacements[None, :])
        & (jnp.arange(momenta.shape[0])[None, :] < jnp.arange(momenta.shape[0])[:, None]),
        axis=1,
    ).astype(jnp.int32)
    source = slot + len(values) * (seen != side).astype(jnp.int32)
    rows = jnp.take(both, source, axis=0)
    return (rows[None], correlators[:, None, :])


def solution(mesh):
    return jax.shard_map(
        body,
        mesh=mesh,
        in_specs=(
            P(("cfg", "tm"), None, None, "space", None, None, None),
            P(("cfg", "tm"), None, None, None, None, "space", None, None),
            P(("cfg", "tm"), None, None, None, None),
            P(),
            P(),
        ),
        out_specs=(P(("cfg", "tm"), None, "space", None), P(None, ("cfg", "tm"), None)),
        check_vma=False,
    )
```

```python
import functools
import math

import jax
import jax.numpy as jnp
from jax import lax
from jax.experimental import pallas as pl
from jax.experimental.pallas import tpu as pltpu
from jax.sharding import PartitionSpec as P

ROWS = 16
UNROLL = 8
VALUES = (2, 3, 1, 0)


def pick_operator(disp_ref, value, last):
    count = disp_ref.shape[0]
    first_seen = jnp.int32(count)
    last_seen = jnp.int32(-1)
    for o in range(count):
        hit = disp_ref[o] == value
        first_seen = jnp.where(hit, jnp.minimum(first_seen, o), first_seen)
        last_seen = jnp.where(hit, o, last_seen)
    return jnp.where(last == 0, first_seen, last_seen)


def link_product(entry, field, adjoint):
    real_rows, imag_rows = [], []
    for a in range(3):
        real_sum = imag_sum = None
        for b in range(3):
            if adjoint:
                u_real, u_imag = entry(0, b, a), entry(1, b, a)
                real_term = u_real * field[b] + u_imag * field[3 + b]
                imag_term = u_real * field[3 + b] - u_imag * field[b]
            else:
                u_real, u_imag = entry(0, a, b), entry(1, a, b)
                real_term = u_real * field[b] - u_imag * field[3 + b]
                imag_term = u_real * field[3 + b] + u_imag * field[b]
            real_sum = real_term if real_sum is None else real_sum + real_term
            imag_sum = imag_term if imag_sum is None else imag_sum + imag_term
        real_rows.append(real_sum)
        imag_rows.append(imag_sum)
    return real_rows + imag_rows


def elemental_kernel(
    norm_factor,
    disp_hbm,
    mom_hbm,
    own_hbm,
    other_hbm,
    own_links_hbm,
    other_links_hbm,
    phi_ref,
    disp_ref,
    mom_ref,
    own_ref,
    other_ref,
    own_links_ref,
    other_links_ref,
    vt_ref,
    links_ref,
    back_ref,
    left_ref,
    right_ref,
    sems,
):
    half_x, ny, nz, eigen = own_ref.shape[1:]
    nx = 2 * half_x
    lanes = nx * nz
    count = len(VALUES)
    side = lax.axis_index("space")
    z_at = lax.broadcasted_iota(jnp.int32, (ROWS, lanes), 1) % nz
    pairs = (
        (disp_hbm, disp_ref),
        (mom_hbm, mom_ref),
        (own_links_hbm, own_links_ref),
        (other_links_hbm, other_links_ref),
        (own_hbm, own_ref),
        (other_hbm, other_ref),
    )
    copies = [pltpu.make_async_copy(s, d, sems.at[k]) for k, (s, d) in enumerate(pairs)]
    for copy in copies:
        copy.start()

    def z_ahead(value):
        return jnp.where(
            z_at[: value.shape[0]] == nz - 1,
            pltpu.roll(value, nz - 1, 1),
            pltpu.roll(value, lanes - 1, 1),
        )

    def z_behind(value):
        return jnp.where(
            z_at[: value.shape[0]] == 0,
            pltpu.roll(value, lanes - (nz - 1), 1),
            pltpu.roll(value, 1, 1),
        )

    copies[0].wait()
    copies[1].wait()
    kinds = 2 * count
    operators = disp_ref.shape[1]
    row = lax.broadcasted_iota(jnp.int32, (kinds, operators), 0)
    at = lax.broadcasted_iota(jnp.int32, (kinds, operators), 1).astype(jnp.float32)
    value = jnp.zeros((kinds, operators), jnp.int32)
    for slot, wanted in enumerate(VALUES):
        value = jnp.where(row // 2 == slot, wanted, value)
    hit = jnp.broadcast_to(disp_ref[...], (kinds, operators)) == value
    first = jnp.min(jnp.where(hit, at, operators), axis=1, keepdims=True)
    last = jnp.max(jnp.where(hit, at, -1.0), axis=1, keepdims=True)
    chosen = at == jnp.where(side == 0, first, last)
    momenta = mom_ref[...].astype(jnp.float32)
    steps = []
    for k, scale in enumerate((nz // nx, nz // ny, 1)):
        spread_out = jnp.broadcast_to(momenta[k : k + 1], (kinds, operators))
        total = jnp.sum(jnp.where(chosen, spread_out, 0.0), axis=1, keepdims=True)
        steps.append(total.astype(jnp.int32) * scale)
    lane = lax.broadcasted_iota(jnp.int32, (kinds, lanes), 1)
    kind = lax.broadcasted_iota(jnp.int32, (kinds, lanes), 0)
    x_true = (lane // nz + half_x * side) % nx
    plane = steps[0] * x_true + steps[2] * (lane % nz) - (kind % 2) * (nz // 4)
    waves = []
    for y in range(ny):
        turns = ((plane + steps[1] * y + nz // 2) & (nz - 1)) - nz // 2
        waves.append(jnp.cos(turns.astype(jnp.float32) * (2.0 * math.pi / nz)).T)

    copies[2].wait()
    copies[3].wait()
    pieces = [own_links_ref[:, x] for x in range(half_x)]
    pieces += [other_links_ref[:, x] for x in range(half_x)]
    links = jnp.concatenate(pieces, axis=-1)
    links_ref[...] = links
    for row in range(18):
        back_ref[row] = pltpu.roll(links[row], nz, 1)
        back_ref[18 + row] = z_behind(links[36 + row])

    copies[4].wait()
    copies[5].wait()

    def lay_out(y):
        field = []
        for c in range(6):
            blocks = [own_ref[c, x, y] for x in range(half_x)]
            blocks += [other_ref[c, x, y] for x in range(half_x)]
            field.append(jnp.concatenate(blocks, axis=0).astype(jnp.float32))
            vt_ref[c, y] = field[c].T
        for slot in range(count):
            cosine = jnp.broadcast_to(waves[y][:, 2 * slot : 2 * slot + 1], (lanes, eigen))
            sine = jnp.broadcast_to(waves[y][:, 2 * slot + 1 : 2 * slot + 2], (lanes, eigen))
            for a in range(3):
                real = field[a] * cosine - field[3 + a] * sine
                imag = field[a] * sine + field[3 + a] * cosine
                base = (y * 6 + 2 * a) * lanes
                left_ref[slot, pl.ds(base, lanes), :] = real.astype(jnp.bfloat16)
                left_ref[slot, pl.ds(base + lanes, lanes), :] = imag.astype(jnp.bfloat16)

    def fields(y):
        y_ahead = (y + 1) % ny
        y_behind = (y + ny - 1) % ny

        def chunk(e):
            rows = pl.ds(pl.multiple_of(e * ROWS, ROWS), ROWS)
            lower = pl.ds(pl.multiple_of(e * ROWS + eigen, ROWS), ROWS)

            def entries(ref, base, at):
                return lambda part, a, b: ref[base + part * 9 + a * 3 + b, pl.ds(at, 1), :]

            def put(value, moved):
                slot = VALUES.index(value)
                for a in range(3):
                    even = pl.ds((y * 6 + 2 * a) * lanes, lanes)
                    odd = pl.ds((y * 6 + 2 * a + 1) * lanes, lanes)
                    real = moved[a].astype(jnp.bfloat16)
                    imag = moved[3 + a].astype(jnp.bfloat16)
                    right_ref[slot, rows, even] = real
                    right_ref[slot, rows, odd] = imag
                    right_ref[slot, lower, even] = imag
                    right_ref[slot, lower, odd] = -real

            field = [vt_ref[c, y, rows, :] for c in range(6)]
            ahead = [pltpu.roll(f, lanes - nz, 1) for f in field]
            moved = link_product(entries(links_ref, 0, y), ahead, False)
            put(1, moved)
            total = moved
            ahead = [vt_ref[c, y_ahead, rows, :] for c in range(6)]
            moved = link_product(entries(links_ref, 18, y), ahead, False)
            put(2, moved)
            total = [p + q for p, q in zip(total, moved)]
            ahead = [z_ahead(f) for f in field]
            moved = link_product(entries(links_ref, 36, y), ahead, False)
            put(3, moved)
            total = [p + q for p, q in zip(total, moved)]
            behind = [pltpu.roll(f, nz, 1) for f in field]
            moved = link_product(entries(back_ref, 0, y), behind, True)
            total = [p + q for p, q in zip(total, moved)]
            behind = [vt_ref[c, y_behind, rows, :] for c in range(6)]
            moved = link_product(entries(links_ref, 18, y_behind), behind, True)
            total = [p + q for p, q in zip(total, moved)]
            behind = [z_behind(f) for f in field]
            moved = link_product(entries(back_ref, 18, y), behind, True)
            total = [p + q for p, q in zip(total, moved)]
            put(0, [f - t * (1.0 / 6.0) for f, t in zip(field, total)])

        lax.fori_loop(0, eigen // ROWS, lambda e, c: (chunk(e), c)[1], 0, unroll=UNROLL)

    for y in range(ny):
        lay_out(y)
    for y in range(ny):
        fields(y)
    for slot in range(count):
        total = jnp.dot(right_ref[slot], left_ref[slot], preferred_element_type=jnp.float32)
        total = (total * norm_factor).astype(jnp.bfloat16)
        phi_ref[slot] = jnp.concatenate([total[:eigen], total[eigen:]], axis=1)


def elementals(norm_factor, displacements, momenta, own, other, own_links, other_links):
    half_x, ny, nz, eigen = own.shape[1:]
    lanes = 2 * half_x * nz
    count = len(VALUES)
    vmem = pl.BlockSpec(memory_space=pltpu.VMEM)
    anywhere = pl.BlockSpec(memory_space=pl.ANY)
    operands = (displacements, momenta, own, other, own_links, other_links)
    return pl.pallas_call(
        functools.partial(elemental_kernel, norm_factor),
        out_shape=jax.ShapeDtypeStruct((count, eigen, 2 * eigen), jnp.bfloat16),
        in_specs=[anywhere] * 6,
        out_specs=vmem,
        scratch_shapes=[pltpu.VMEM(p.shape, p.dtype) for p in operands]
        + [
            pltpu.VMEM((6, ny, eigen, lanes), jnp.float32),
            pltpu.VMEM((54, ny, lanes), jnp.float32),
            pltpu.VMEM((36, ny, lanes), jnp.float32),
            pltpu.VMEM((count, 6 * ny * lanes, eigen), jnp.bfloat16),
            pltpu.VMEM((count, 2 * eigen, 6 * ny * lanes), jnp.bfloat16),
            pltpu.SemaphoreType.DMA((6,)),
        ],
        compiler_params=pltpu.CompilerParams(vmem_limit_bytes=40 * 1024 * 1024),
        cost_estimate=pl.CostEstimate(
            flops=count * 2 * 6 * ny * lanes * eigen * 2 * eigen,
            bytes_accessed=2 * own.size * 2,
            transcendentals=0,
        ),
        name="elementals",
    )(*operands)


def separation(index, ring):
    if not ring:
        return jnp.int32(index)
    count = lax.axis_size("tm")
    me = lax.axis_index("tm")
    place = jnp.where(me % 2 == 0, me // 2, count - (me + 1) // 2)
    hops = (index + 1) // 2 if index % 2 == 1 else -(index // 2)
    at = (place - hops + count) % count
    owner = jnp.where(at < count // 2, 2 * at, 2 * (count - at) - 1)
    return (me - owner + count) % count


def add_to_table(table, product, slot, column):
    total = jnp.sum(jnp.sum(product, axis=0, keepdims=True), axis=1, keepdims=True)
    total = total * (1.0 / product.shape[0])
    row_at = lax.broadcasted_iota(jnp.int32, table.shape, 0)
    column_at = lax.broadcasted_iota(jnp.int32, table.shape, 1)
    return table + jnp.where((row_at == slot) & (column_at == column), total, 0.0)


def sandwich_kernel(made, met, halves, ring, *refs):
    refs = list(refs)
    table_ref = refs.pop(0)
    if made:
        phi_ref, peram_hbm = refs.pop(0), refs.pop(0)
    if met:
        before_ref = refs.pop(0)
        arrival_refs = [refs.pop(0) for _ in range(2 if halves else len(met))]
    table_out = refs.pop(0)
    if made:
        out_ref, peram_ref, mixed_ref, sems = refs
        copies = []
        for k, index in enumerate(made):
            copy = pltpu.make_async_copy(
                peram_hbm.at[separation(index, ring)], peram_ref.at[k], sems.at[k]
            )
            copy.start()
            copies.append(copy)
    table = table_ref[...]
    if met:
        slots, eigen = before_ref.shape[1:3]
        for k, index in enumerate(met):
            column = separation(index, ring)
            for slot in range(slots):
                if halves:
                    rows = arrival_refs[slot // (slots // 2)][slot % (slots // 2)]
                else:
                    rows = arrival_refs[k][slot]
                product = rows.astype(jnp.float32) * before_ref[k, slot]
                table = add_to_table(table, product, slot, column)
    if made:
        slots, eigen, _ = phi_ref.shape
        spins = peram_ref.shape[1]
        blocks = []
        for slot in range(slots):
            rows = phi_ref[slot]
            turned = jnp.concatenate([-rows[:, eigen:], rows[:, :eigen]], axis=1)
            blocks.append(jnp.concatenate([rows, turned], axis=0))
        for k, index in enumerate(made):
            copies[k].wait()
            flipped, weights = [], []
            for a in range(spins):
                peram = peram_ref[k, a]
                real, imag = peram[:, :eigen], peram[:, eigen:]
                flipped.append(jnp.concatenate([real.T, imag.T], axis=1))
                weights.append(jnp.concatenate([real, -imag], axis=1))
                weights.append(jnp.concatenate([imag, real], axis=1))
            flipped = jnp.concatenate(flipped, axis=0)
            weights = jnp.concatenate(weights, axis=0)
            for slot in range(slots):
                mixed = jnp.dot(flipped, blocks[slot], preferred_element_type=jnp.float32)
                mixed = mixed.astype(jnp.bfloat16)
                for a in range(spins):
                    mixed_ref[
                        slot * eigen : (slot + 1) * eigen, 2 * eigen * a : 2 * eigen * (a + 1)
                    ] = mixed[a * eigen : (a + 1) * eigen]
            result = jnp.dot(mixed_ref[...], weights, preferred_element_type=jnp.float32)
            result = result.reshape(slots, eigen, 2 * eigen)
            if index == 0:
                for slot in range(slots):
                    product = phi_ref[slot].astype(jnp.float32) * result[slot]
                    table = add_to_table(table, product, slot, 0)
            else:
                out_ref[k - (made[0] == 0)] = result
    table_out[...] = table


def sandwich_step(table, phi, perambulators, made, before, arrivals, met, ring):
    slots, eigen, columns = phi.shape
    separations, spins = perambulators.shape[:2]
    vmem = pl.BlockSpec(memory_space=pltpu.VMEM)
    halves = len(arrivals) > len(met)
    operands, specs = [table], [vmem]
    shapes, scratch = [jax.ShapeDtypeStruct(table.shape, table.dtype)], []
    if made:
        operands += [phi, perambulators]
        specs += [vmem, pl.BlockSpec(memory_space=pl.ANY)]
        kept = len([k for k in made if k > 0])
        shapes.append(jax.ShapeDtypeStruct((kept, slots, eigen, columns), jnp.float32))
        scratch = [
            pltpu.VMEM((len(made),) + perambulators.shape[1:], perambulators.dtype),
            pltpu.VMEM((slots * eigen, spins * columns), jnp.bfloat16),
            pltpu.SemaphoreType.DMA((len(made),)),
        ]
    if met:
        operands += [before] + list(arrivals)
        specs += [vmem] * (1 + len(arrivals))
    work = 4 * spins * slots * eigen * columns * columns
    return pl.pallas_call(
        functools.partial(sandwich_kernel, tuple(made), tuple(met), halves, ring),
        out_shape=tuple(shapes),
        in_specs=specs,
        out_specs=(vmem,) * len(shapes),
        scratch_shapes=scratch,
        compiler_params=pltpu.CompilerParams(vmem_limit_bytes=24 * 1024 * 1024),
        cost_estimate=pl.CostEstimate(
            flops=len(made) * work + 1000,
            bytes_accessed=len(made) * 2 * spins * eigen * columns + 1000,
            transcendentals=0,
        ),
        name="sandwich" + "".join(str(k) for k in made) + "_meet" + "".join(str(k) for k in met),
    )(*operands)


def turn_kernel(phi_ref, kept_ref, given_ref, whole_ref):
    slots, eigen, _ = phi_ref.shape
    half = eigen // 2
    side = lax.axis_index("space")
    for slot in range(slots):
        rows = phi_ref[slot]
        whole_ref[slot] = jnp.concatenate([rows[:, :eigen].T, rows[:, eigen:].T], axis=1)
    mine = pl.ds(pl.multiple_of(side * half, half), half)
    others = pl.ds(pl.multiple_of((1 - side) * half, half), half)
    kept_ref[...] = whole_ref[:, mine, :]
    given_ref[...] = whole_ref[:, others, :]


def turn(phi):
    slots, eigen, columns = phi.shape
    vmem = pl.BlockSpec(memory_space=pltpu.VMEM)
    half = jax.ShapeDtypeStruct((slots, eigen // 2, columns), phi.dtype)
    return pl.pallas_call(
        turn_kernel,
        out_shape=(half, half),
        in_specs=[vmem],
        out_specs=(vmem, vmem),
        scratch_shapes=[pltpu.VMEM(phi.shape, phi.dtype)],
        cost_estimate=pl.CostEstimate(flops=1000, bytes_accessed=4 * phi.size, transcendentals=0),
        name="turn",
    )(phi)


def order_kernel(source_ref, kept_ref, taken_ref, out_ref):
    slots = kept_ref.shape[0]
    for o in range(out_ref.shape[0]):
        at = source_ref[o]

        @pl.when(at < slots)
        def _(at=at, o=o):
            out_ref[o] = kept_ref[at]

        @pl.when(at >= slots)
        def _(at=at, o=o):
            out_ref[o] = taken_ref[at - slots]


def order(source, kept, taken):
    vmem = pl.BlockSpec(memory_space=pltpu.VMEM)
    shape = (2 * kept.shape[0],) + kept.shape[1:]
    return pl.pallas_call(
        order_kernel,
        out_shape=jax.ShapeDtypeStruct(shape, kept.dtype),
        in_specs=[pl.BlockSpec(memory_space=pltpu.SMEM), vmem, vmem],
        out_specs=vmem,
        cost_estimate=pl.CostEstimate(flops=1000, bytes_accessed=8 * kept.size, transcendentals=0),
        name="order",
    )(source, kept, taken)


def body(vectors, gauge_links, perambulators, momenta, displacements):
    side = lax.axis_index("space")
    swap = [(0, 1), (1, 0)]
    half_x, ny, nz, eigen = vectors.shape[3:]
    own = vectors.reshape((6, half_x, ny, nz, eigen))
    own_links = gauge_links.reshape((54, half_x, ny, nz))
    other = lax.ppermute(own, "space", swap)
    other_links = lax.ppermute(own_links, "space", swap)
    norm_factor = 1.0 / math.sqrt(6.0 * 2 * half_x * ny * nz)
    operators = momenta.shape[0]
    phi = elementals(
        norm_factor, displacements.reshape((1, operators)), momenta.T, own, other, own_links, other_links
    )
    slots = phi.shape[0]

    count = lax.axis_size("tm")
    peram = perambulators[0]
    separations = peram.shape[0]
    ring = count == separations
    if ring:
        around = list(range(0, count, 2)) + list(range(count - 1, 0, -2))
        ahead = [(around[k], around[(k + 1) % count]) for k in range(count)]
        behind = [(b, a) for a, b in ahead]
        one_way = [phi]
        other_way = [phi]
        arrivals = [None]
        for _ in range((separations - 2) // 2):
            one_way.append(lax.ppermute(one_way[-1], "tm", ahead))
            other_way.append(lax.ppermute(other_way[-1], "tm", behind))
            arrivals += [one_way[-1], other_way[-1]]
        last = [
            lax.ppermute(one_way[-1][: slots // 2], "tm", ahead),
            lax.ppermute(other_way[-1][slots // 2 :], "tm", behind),
        ]
    else:
        arrivals = [phi]
        for _ in range(separations - 1):
            arrivals.append(lax.ppermute(arrivals[-1], "tm", [(i, (i + 1) % count) for i in range(count)]))
        last = [arrivals[-1][: slots // 2], arrivals[-1][slots // 2 :]]

    table = jnp.zeros((slots, separations), jnp.float32)
    before, met, came = None, [], []
    for first in range(1, separations, 2):
        made = [k for k in (first, first + 1) if k < separations]
        if first == 1:
            made = [0] + made
        table, sands = sandwich_step(table, phi, peram, made, before, came, met, ring)
        before, met = sands, [k for k in made if k > 0]
        came = last if len(met) == 1 else [arrivals[k] for k in met]
    (table,) = sandwich_step(table, phi, peram, [], before, came, met, ring)
    other_table = lax.ppermute(table, "space", swap)

    number = jnp.arange(operators)
    earlier = (displacements[:, None] == displacements[None, :]) & (number[None, :] < number[:, None])
    mine = jnp.sum(earlier.astype(jnp.int32), axis=1) == side
    slot_of = jnp.zeros((operators,), jnp.int32)
    for slot, value in enumerate(VALUES):
        slot_of = jnp.where(displacements == value, slot, slot_of)
    source = slot_of + jnp.where(mine, 0, slots)
    own_place = (source[:, None] == jnp.arange(slots)[None, :])[:, :, None]
    other_place = (source[:, None] == slots + jnp.arange(slots)[None, :])[:, :, None]
    correlators = jnp.sum(
        jnp.where(own_place, table[None], 0.0) + jnp.where(other_place, other_table[None], 0.0), axis=1
    )
    kept, given = turn(phi)
    taken = lax.ppermute(given, "space", swap)
    rows = order(source, kept, taken)
    return (rows[None], correlators[:, None, :])


def solution(mesh):
    return jax.shard_map(
        body,
        mesh=mesh,
        in_specs=(
            P(("cfg", "tm"), None, None, "space", None, None, None),
            P(("cfg", "tm"), None, None, None, None, "space", None, None),
            P(("cfg", "tm"), None, None, None, None),
            P(),
            P(),
        ),
        out_specs=(P(("cfg", "tm"), None, "space", None), P(None, ("cfg", "tm"), None)),
        check_vma=False,
    )
```

```python
import functools
import math

import jax
import jax.numpy as jnp
from jax import lax
from jax.experimental import pallas as pl
from jax.experimental.pallas import tpu as pltpu
from jax.sharding import PartitionSpec as P

ROWS = 16
UNROLL = 8
VALUES = (2, 3, 1, 0)


def pick_operator(disp_ref, value, last):
    count = disp_ref.shape[0]
    first_seen = jnp.int32(count)
    last_seen = jnp.int32(-1)
    for o in range(count):
        hit = disp_ref[o] == value
        first_seen = jnp.where(hit, jnp.minimum(first_seen, o), first_seen)
        last_seen = jnp.where(hit, o, last_seen)
    return jnp.where(last == 0, first_seen, last_seen)


def link_product(entry, field, adjoint):
    real_rows, imag_rows = [], []
    for a in range(3):
        real_sum = imag_sum = None
        for b in range(3):
            if adjoint:
                u_real, u_imag = entry(0, b, a), entry(1, b, a)
                real_term = u_real * field[b] + u_imag * field[3 + b]
                imag_term = u_real * field[3 + b] - u_imag * field[b]
            else:
                u_real, u_imag = entry(0, a, b), entry(1, a, b)
                real_term = u_real * field[b] - u_imag * field[3 + b]
                imag_term = u_real * field[3 + b] + u_imag * field[b]
            real_sum = real_term if real_sum is None else real_sum + real_term
            imag_sum = imag_term if imag_sum is None else imag_sum + imag_term
        real_rows.append(real_sum)
        imag_rows.append(imag_sum)
    return real_rows + imag_rows


def elemental_kernel(
    norm_factor,
    disp_hbm,
    mom_hbm,
    own_hbm,
    other_hbm,
    own_links_hbm,
    other_links_hbm,
    phi_ref,
    disp_ref,
    mom_ref,
    own_ref,
    other_ref,
    own_links_ref,
    other_links_ref,
    vt_ref,
    links_ref,
    back_ref,
    left_ref,
    right_ref,
    sems,
):
    half_x, ny, nz, eigen = own_ref.shape[1:]
    nx = 2 * half_x
    lanes = nx * nz
    count = len(VALUES)
    side = lax.axis_index("space")
    z_at = lax.broadcasted_iota(jnp.int32, (ROWS, lanes), 1) % nz
    pairs = (
        (disp_hbm, disp_ref),
        (mom_hbm, mom_ref),
        (own_links_hbm, own_links_ref),
        (other_links_hbm, other_links_ref),
        (own_hbm, own_ref),
        (other_hbm, other_ref),
    )
    copies = [pltpu.make_async_copy(s, d, sems.at[k]) for k, (s, d) in enumerate(pairs)]
    for copy in copies:
        copy.start()

    def z_ahead(value):
        return jnp.where(
            z_at[: value.shape[0]] == nz - 1,
            pltpu.roll(value, nz - 1, 1),
            pltpu.roll(value, lanes - 1, 1),
        )

    def z_behind(value):
        return jnp.where(
            z_at[: value.shape[0]] == 0,
            pltpu.roll(value, lanes - (nz - 1), 1),
            pltpu.roll(value, 1, 1),
        )

    copies[0].wait()
    copies[1].wait()
    kinds = 2 * count
    operators = disp_ref.shape[1]
    row = lax.broadcasted_iota(jnp.int32, (kinds, operators), 0)
    at = lax.broadcasted_iota(jnp.int32, (kinds, operators), 1).astype(jnp.float32)
    value = jnp.zeros((kinds, operators), jnp.int32)
    for slot, wanted in enumerate(VALUES):
        value = jnp.where(row // 2 == slot, wanted, value)
    hit = jnp.broadcast_to(disp_ref[...], (kinds, operators)) == value
    first = jnp.min(jnp.where(hit, at, operators), axis=1, keepdims=True)
    last = jnp.max(jnp.where(hit, at, -1.0), axis=1, keepdims=True)
    chosen = at == jnp.where(side == 0, first, last)
    momenta = mom_ref[...].astype(jnp.float32)
    steps = []
    for k, scale in enumerate((nz // nx, nz // ny, 1)):
        spread_out = jnp.broadcast_to(momenta[k : k + 1], (kinds, operators))
        total = jnp.sum(jnp.where(chosen, spread_out, 0.0), axis=1, keepdims=True)
        steps.append(total.astype(jnp.int32) * scale)
    lane = lax.broadcasted_iota(jnp.int32, (kinds, lanes), 1)
    kind = lax.broadcasted_iota(jnp.int32, (kinds, lanes), 0)
    x_true = (lane // nz + half_x * side) % nx
    plane = steps[0] * x_true + steps[2] * (lane % nz) - (kind % 2) * (nz // 4)
    waves = []
    for y in range(ny):
        turns = ((plane + steps[1] * y + nz // 2) & (nz - 1)) - nz // 2
        waves.append(jnp.cos(turns.astype(jnp.float32) * (2.0 * math.pi / nz)).T)

    copies[2].wait()
    copies[3].wait()
    pieces = [own_links_ref[:, x] for x in range(half_x)]
    pieces += [other_links_ref[:, x] for x in range(half_x)]
    links = jnp.concatenate(pieces, axis=-1)
    links_ref[...] = links
    for row in range(18):
        back_ref[row] = pltpu.roll(links[row], nz, 1)
        back_ref[18 + row] = z_behind(links[36 + row])

    copies[4].wait()
    copies[5].wait()

    def lay_out(y):
        field = []
        for c in range(6):
            blocks = [own_ref[c, x, y] for x in range(half_x)]
            blocks += [other_ref[c, x, y] for x in range(half_x)]
            field.append(jnp.concatenate(blocks, axis=0).astype(jnp.float32))
            vt_ref[c, y] = field[c].T
        for slot in range(count):
            cosine = jnp.broadcast_to(waves[y][:, 2 * slot : 2 * slot + 1], (lanes, eigen))
            sine = jnp.broadcast_to(waves[y][:, 2 * slot + 1 : 2 * slot + 2], (lanes, eigen))
            for a in range(3):
                real = field[a] * cosine - field[3 + a] * sine
                imag = field[a] * sine + field[3 + a] * cosine
                base = (y * 6 + 2 * a) * lanes
                left_ref[slot, pl.ds(base, lanes), :] = real.astype(jnp.bfloat16)
                left_ref[slot, pl.ds(base + lanes, lanes), :] = imag.astype(jnp.bfloat16)

    def fields(y):
        y_ahead = (y + 1) % ny
        y_behind = (y + ny - 1) % ny

        def chunk(e):
            rows = pl.ds(pl.multiple_of(e * ROWS, ROWS), ROWS)
            lower = pl.ds(pl.multiple_of(e * ROWS + eigen, ROWS), ROWS)

            def entries(ref, base, at):
                return lambda part, a, b: ref[base + part * 9 + a * 3 + b, pl.ds(at, 1), :]

            def put(value, moved):
                slot = VALUES.index(value)
                for a in range(3):
                    even = pl.ds((y * 6 + 2 * a) * lanes, lanes)
                    odd = pl.ds((y * 6 + 2 * a + 1) * lanes, lanes)
                    real = moved[a].astype(jnp.bfloat16)
                    imag = moved[3 + a].astype(jnp.bfloat16)
                    right_ref[slot, rows, even] = real
                    right_ref[slot, rows, odd] = imag
                    right_ref[slot, lower, even] = imag
                    right_ref[slot, lower, odd] = -real

            field = [vt_ref[c, y, rows, :] for c in range(6)]
            ahead = [pltpu.roll(f, lanes - nz, 1) for f in field]
            moved = link_product(entries(links_ref, 0, y), ahead, False)
            put(1, moved)
            total = moved
            ahead = [vt_ref[c, y_ahead, rows, :] for c in range(6)]
            moved = link_product(entries(links_ref, 18, y), ahead, False)
            put(2, moved)
            total = [p + q for p, q in zip(total, moved)]
            ahead = [z_ahead(f) for f in field]
            moved = link_product(entries(links_ref, 36, y), ahead, False)
            put(3, moved)
            total = [p + q for p, q in zip(total, moved)]
            behind = [pltpu.roll(f, nz, 1) for f in field]
            moved = link_product(entries(back_ref, 0, y), behind, True)
            total = [p + q for p, q in zip(total, moved)]
            behind = [vt_ref[c, y_behind, rows, :] for c in range(6)]
            moved = link_product(entries(links_ref, 18, y_behind), behind, True)
            total = [p + q for p, q in zip(total, moved)]
            behind = [z_behind(f) for f in field]
            moved = link_product(entries(back_ref, 18, y), behind, True)
            total = [p + q for p, q in zip(total, moved)]
            put(0, [f - t * (1.0 / 6.0) for f, t in zip(field, total)])

        lax.fori_loop(0, eigen // ROWS, lambda e, c: (chunk(e), c)[1], 0, unroll=UNROLL)

    for y in range(ny):
        lay_out(y)
    for y in range(ny):
        fields(y)
    for slot in range(count):
        total = jnp.dot(right_ref[slot], left_ref[slot], preferred_element_type=jnp.float32)
        total = (total * norm_factor).astype(jnp.bfloat16)
        phi_ref[slot] = jnp.concatenate([total[:eigen], total[eigen:]], axis=1)


def elementals(norm_factor, displacements, momenta, own, other, own_links, other_links):
    half_x, ny, nz, eigen = own.shape[1:]
    lanes = 2 * half_x * nz
    count = len(VALUES)
    vmem = pl.BlockSpec(memory_space=pltpu.VMEM)
    anywhere = pl.BlockSpec(memory_space=pltpu.HBM)
    operands = (displacements, momenta, own, other, own_links, other_links)
    return pl.pallas_call(
        functools.partial(elemental_kernel, norm_factor),
        out_shape=jax.ShapeDtypeStruct((count, eigen, 2 * eigen), jnp.bfloat16),
        in_specs=[anywhere] * 6,
        out_specs=vmem,
        scratch_shapes=[pltpu.VMEM(p.shape, p.dtype) for p in operands]
        + [
            pltpu.VMEM((6, ny, eigen, lanes), jnp.float32),
            pltpu.VMEM((54, ny, lanes), jnp.float32),
            pltpu.VMEM((36, ny, lanes), jnp.float32),
            pltpu.VMEM((count, 6 * ny * lanes, eigen), jnp.bfloat16),
            pltpu.VMEM((count, 2 * eigen, 6 * ny * lanes), jnp.bfloat16),
            pltpu.SemaphoreType.DMA((6,)),
        ],
        compiler_params=pltpu.CompilerParams(vmem_limit_bytes=60 * 1024 * 1024),
        cost_estimate=pl.CostEstimate(
            flops=count * 2 * 6 * ny * lanes * eigen * 2 * eigen,
            bytes_accessed=2 * own.size * 2,
            transcendentals=0,
        ),
        name="elementals",
    )(*operands)


def separation(index, ring):
    if not ring:
        return jnp.int32(index)
    count = lax.axis_size("tm")
    me = lax.axis_index("tm")
    place = jnp.where(me % 2 == 0, me // 2, count - (me + 1) // 2)
    hops = (index + 1) // 2 if index % 2 == 1 else -(index // 2)
    at = (place - hops + count) % count
    owner = jnp.where(at < count // 2, 2 * at, 2 * (count - at) - 1)
    return (me - owner + count) % count


def add_to_table(table, product, slot, column):
    total = jnp.sum(jnp.sum(product, axis=0, keepdims=True), axis=1, keepdims=True)
    total = total * (1.0 / product.shape[0])
    row_at = lax.broadcasted_iota(jnp.int32, table.shape, 0)
    column_at = lax.broadcasted_iota(jnp.int32, table.shape, 1)
    return table + jnp.where((row_at == slot) & (column_at == column), total, 0.0)


def sandwich_kernel(made, met, halves, ring, *refs):
    refs = list(refs)
    table_ref = refs.pop(0)
    if made:
        phi_ref, peram_hbm = refs.pop(0), refs.pop(0)
    if met:
        before_ref = refs.pop(0)
        arrival_refs = [refs.pop(0) for _ in range(2 if halves else len(met))]
    table_out = refs.pop(0)
    if made:
        out_ref, peram_ref, mixed_ref, sems = refs
        copies = []
        for k, index in enumerate(made):
            copy = pltpu.make_async_copy(
                peram_hbm.at[separation(index, ring)], peram_ref.at[k], sems.at[k]
            )
            copy.start()
            copies.append(copy)
    table = table_ref[...]
    if met:
        slots, eigen = before_ref.shape[1:3]
        for k, index in enumerate(met):
            column = separation(index, ring)
            for slot in range(slots):
                if halves:
                    rows = arrival_refs[slot // (slots // 2)][slot % (slots // 2)]
                else:
                    rows = arrival_refs[k][slot]
                product = rows.astype(jnp.float32) * before_ref[k, slot]
                table = add_to_table(table, product, slot, column)
    if made:
        slots, eigen, _ = phi_ref.shape
        spins = peram_ref.shape[1]
        blocks = []
        for slot in range(slots):
            rows = phi_ref[slot]
            turned = jnp.concatenate([-rows[:, eigen:], rows[:, :eigen]], axis=1)
            blocks.append(jnp.concatenate([rows, turned], axis=0))
        for k, index in enumerate(made):
            copies[k].wait()
            flipped, weights = [], []
            for a in range(spins):
                peram = peram_ref[k, a]
                real, imag = peram[:, :eigen], peram[:, eigen:]
                flipped.append(jnp.concatenate([real.T, imag.T], axis=1))
                weights.append(jnp.concatenate([real, -imag], axis=1))
                weights.append(jnp.concatenate([imag, real], axis=1))
            flipped = jnp.concatenate(flipped, axis=0)
            weights = jnp.concatenate(weights, axis=0)
            for slot in range(slots):
                mixed = jnp.dot(flipped, blocks[slot], preferred_element_type=jnp.float32)
                mixed = mixed.astype(jnp.bfloat16)
                for a in range(spins):
                    mixed_ref[
                        slot * eigen : (slot + 1) * eigen, 2 * eigen * a : 2 * eigen * (a + 1)
                    ] = mixed[a * eigen : (a + 1) * eigen]
            result = jnp.dot(mixed_ref[...], weights, preferred_element_type=jnp.float32)
            result = result.reshape(slots, eigen, 2 * eigen)
            if index == 0:
                for slot in range(slots):
                    product = phi_ref[slot].astype(jnp.float32) * result[slot]
                    table = add_to_table(table, product, slot, 0)
            else:
                out_ref[k - (made[0] == 0)] = result
    table_out[...] = table


def sandwich_step(table, phi, perambulators, made, before, arrivals, met, ring):
    slots, eigen, columns = phi.shape
    separations, spins = perambulators.shape[:2]
    vmem = pl.BlockSpec(memory_space=pltpu.VMEM)
    halves = len(arrivals) > len(met)
    operands, specs = [table], [vmem]
    shapes, scratch = [jax.ShapeDtypeStruct(table.shape, table.dtype)], []
    if made:
        operands += [phi, perambulators]
        specs += [vmem, pl.BlockSpec(memory_space=pltpu.HBM)]
        kept = len([k for k in made if k > 0])
        shapes.append(jax.ShapeDtypeStruct((kept, slots, eigen, columns), jnp.float32))
        scratch = [
            pltpu.VMEM((len(made),) + perambulators.shape[1:], perambulators.dtype),
            pltpu.VMEM((slots * eigen, spins * columns), jnp.bfloat16),
            pltpu.SemaphoreType.DMA((len(made),)),
        ]
    if met:
        operands += [before] + list(arrivals)
        specs += [vmem] * (1 + len(arrivals))
    work = 4 * spins * slots * eigen * columns * columns
    return pl.pallas_call(
        functools.partial(sandwich_kernel, tuple(made), tuple(met), halves, ring),
        out_shape=tuple(shapes),
        in_specs=specs,
        out_specs=(vmem,) * len(shapes),
        scratch_shapes=scratch,
        compiler_params=pltpu.CompilerParams(vmem_limit_bytes=24 * 1024 * 1024),
        cost_estimate=pl.CostEstimate(
            flops=len(made) * work + 1000,
            bytes_accessed=len(made) * 2 * spins * eigen * columns + 1000,
            transcendentals=0,
        ),
        name="sandwich" + "".join(str(k) for k in made) + "_meet" + "".join(str(k) for k in met),
    )(*operands)


def turn_kernel(phi_ref, kept_ref, given_ref, whole_ref):
    slots, eigen, _ = phi_ref.shape
    half = eigen // 2
    side = lax.axis_index("space")
    for slot in range(slots):
        rows = phi_ref[slot]
        whole_ref[slot] = jnp.concatenate([rows[:, :eigen].T, rows[:, eigen:].T], axis=1)
    mine = pl.ds(pl.multiple_of(side * half, half), half)
    others = pl.ds(pl.multiple_of((1 - side) * half, half), half)
    kept_ref[...] = whole_ref[:, mine, :]
    given_ref[...] = whole_ref[:, others, :]


def turn(phi):
    slots, eigen, columns = phi.shape
    vmem = pl.BlockSpec(memory_space=pltpu.VMEM)
    half = jax.ShapeDtypeStruct((slots, eigen // 2, columns), phi.dtype)
    return pl.pallas_call(
        turn_kernel,
        out_shape=(half, half),
        in_specs=[vmem],
        out_specs=(vmem, vmem),
        scratch_shapes=[pltpu.VMEM(phi.shape, phi.dtype)],
        cost_estimate=pl.CostEstimate(flops=1000, bytes_accessed=4 * phi.size, transcendentals=0),
        name="turn",
    )(phi)


def order_kernel(source_ref, kept_ref, taken_ref, out_ref):
    slots = kept_ref.shape[0]
    for o in range(out_ref.shape[0]):
        at = source_ref[o]

        @pl.when(at < slots)
        def _(at=at, o=o):
            out_ref[o] = kept_ref[at]

        @pl.when(at >= slots)
        def _(at=at, o=o):
            out_ref[o] = taken_ref[at - slots]


def order(source, kept, taken):
    vmem = pl.BlockSpec(memory_space=pltpu.VMEM)
    shape = (2 * kept.shape[0],) + kept.shape[1:]
    return pl.pallas_call(
        order_kernel,
        out_shape=jax.ShapeDtypeStruct(shape, kept.dtype),
        in_specs=[pl.BlockSpec(memory_space=pltpu.SMEM), vmem, vmem],
        out_specs=vmem,
        cost_estimate=pl.CostEstimate(flops=1000, bytes_accessed=8 * kept.size, transcendentals=0),
        name="order",
    )(source, kept, taken)


def ring_pairs(count):
    around = list(range(0, count, 2)) + list(range(count - 1 - count % 2, 0, -2))
    ahead = [(around[k], around[(k + 1) % count]) for k in range(count)]
    return ahead, [(b, a) for a, b in ahead]


def body(vectors, gauge_links, perambulators, momenta, displacements):
    side = lax.axis_index("space")
    swap = [(0, 1), (1, 0)]
    half_x, ny, nz, eigen = vectors.shape[3:]
    own = vectors.reshape((6, half_x, ny, nz, eigen))
    own_links = gauge_links.reshape((54, half_x, ny, nz))
    other = lax.ppermute(own, "space", swap)
    other_links = lax.ppermute(own_links, "space", swap)
    norm_factor = 1.0 / math.sqrt(6.0 * 2 * half_x * ny * nz)
    operators = momenta.shape[0]
    phi = elementals(
        norm_factor, displacements.reshape((1, operators)), momenta.T, own, other, own_links, other_links
    )
    slots = phi.shape[0]

    count = lax.axis_size("tm")
    peram = perambulators[0]
    separations = peram.shape[0]
    ring = count == separations
    number = jnp.arange(operators)
    earlier = (displacements[:, None] == displacements[None, :]) & (number[None, :] < number[:, None])
    mine = jnp.sum(earlier.astype(jnp.int32), axis=1) == side
    slot_of = jnp.zeros((operators,), jnp.int32)
    for slot, value in enumerate(VALUES):
        slot_of = jnp.where(displacements == value, slot, slot_of)
    source = slot_of + jnp.where(mine, 0, slots)
    own_place = (source[:, None] == jnp.arange(slots)[None, :])[:, :, None]
    other_place = (source[:, None] == slots + jnp.arange(slots)[None, :])[:, :, None]

    table = jnp.zeros((slots, separations), jnp.float32)
    one_way = other_way = phi
    before, met, came = None, [], []
    ahead, behind = ring_pairs(count)
    kept, given = turn(phi)
    for first in range(1, separations, 2):
        made = [k for k in (first, first + 1) if k < separations]
        final = len(made) == 1
        if ring and final:
            arrivals = [
                lax.ppermute(one_way[: slots // 2], "tm", ahead),
                lax.ppermute(other_way[slots // 2 :], "tm", behind),
            ]
        elif ring:
            one_way = lax.ppermute(one_way, "tm", ahead)
            other_way = lax.ppermute(other_way, "tm", behind)
            arrivals = [one_way, other_way]
        else:
            arrivals = []
            for _ in made:
                one_way = lax.ppermute(one_way, "tm", [(i, (i + 1) % count) for i in range(count)])
                arrivals.append(one_way)
            if final:
                arrivals = [one_way[: slots // 2], one_way[slots // 2 :]]
        worked = [0] + made if first == 1 else made
        table, sands = sandwich_step(table, phi, peram, worked, before, came, met, ring)
        before, met, came = sands, made, arrivals
        if first == 1:
            table, kept, given = lax.optimization_barrier((table, kept, given))
            taken = lax.ppermute(given, "space", swap)
        if first == 5:
            rows = order(source, kept, taken)
            table, rows = lax.optimization_barrier((table, rows))
        if not final:
            one_way, other_way, table = lax.optimization_barrier((one_way, other_way, table))
            came = [one_way, other_way] if ring else arrivals
    (table,) = sandwich_step(table, phi, peram, [], before, came, met, ring)
    other_table = lax.ppermute(table, "space", swap)

    correlators = jnp.sum(
        jnp.where(own_place, table[None], 0.0) + jnp.where(other_place, other_table[None], 0.0), axis=1
    )
    return (rows[None], correlators[:, None, :])


def solution(mesh):
    return jax.shard_map(
        body,
        mesh=mesh,
        in_specs=(
            P(("cfg", "tm"), None, None, "space", None, None, None),
            P(("cfg", "tm"), None, None, None, None, "space", None, None),
            P(("cfg", "tm"), None, None, None, None),
            P(),
            P(),
        ),
        out_specs=(P(("cfg", "tm"), None, "space", None), P(None, ("cfg", "tm"), None)),
        check_vma=False,
    )
```

```python
import functools
import math

import jax
import jax.numpy as jnp
from jax import lax
from jax.experimental import pallas as pl
from jax.experimental.pallas import tpu as pltpu
from jax.sharding import PartitionSpec as P

ROWS = 16
UNROLL = 8
VALUES = (2, 3, 1, 0)


def pick_operator(disp_ref, value, last):
    count = disp_ref.shape[0]
    first_seen = jnp.int32(count)
    last_seen = jnp.int32(-1)
    for o in range(count):
        hit = disp_ref[o] == value
        first_seen = jnp.where(hit, jnp.minimum(first_seen, o), first_seen)
        last_seen = jnp.where(hit, o, last_seen)
    return jnp.where(last == 0, first_seen, last_seen)


def link_product(entry, field, adjoint):
    real_rows, imag_rows = [], []
    for a in range(3):
        real_sum = imag_sum = None
        for b in range(3):
            if adjoint:
                u_real, u_imag = entry(0, b, a), entry(1, b, a)
                real_term = u_real * field[b] + u_imag * field[3 + b]
                imag_term = u_real * field[3 + b] - u_imag * field[b]
            else:
                u_real, u_imag = entry(0, a, b), entry(1, a, b)
                real_term = u_real * field[b] - u_imag * field[3 + b]
                imag_term = u_real * field[3 + b] + u_imag * field[b]
            real_sum = real_term if real_sum is None else real_sum + real_term
            imag_sum = imag_term if imag_sum is None else imag_sum + imag_term
        real_rows.append(real_sum)
        imag_rows.append(imag_sum)
    return real_rows + imag_rows


def elemental_kernel(
    norm_factor,
    disp_hbm,
    mom_hbm,
    own_hbm,
    other_hbm,
    own_links_hbm,
    other_links_hbm,
    phi_ref,
    disp_ref,
    mom_ref,
    own_ref,
    other_ref,
    own_links_ref,
    other_links_ref,
    vt_ref,
    links_ref,
    back_ref,
    left_ref,
    right_ref,
    sems,
):
    half_x, ny, nz, eigen = own_ref.shape[1:]
    nx = 2 * half_x
    lanes = nx * nz
    count = len(VALUES)
    side = lax.axis_index("space")
    z_at = lax.broadcasted_iota(jnp.int32, (ROWS, lanes), 1) % nz
    pairs = (
        (disp_hbm, disp_ref),
        (mom_hbm, mom_ref),
        (own_links_hbm, own_links_ref),
        (other_links_hbm, other_links_ref),
        (own_hbm, own_ref),
        (other_hbm, other_ref),
    )
    copies = [pltpu.make_async_copy(s, d, sems.at[k]) for k, (s, d) in enumerate(pairs)]
    for copy in copies:
        copy.start()

    def z_ahead(value):
        return jnp.where(
            z_at[: value.shape[0]] == nz - 1,
            pltpu.roll(value, nz - 1, 1),
            pltpu.roll(value, lanes - 1, 1),
        )

    def z_behind(value):
        return jnp.where(
            z_at[: value.shape[0]] == 0,
            pltpu.roll(value, lanes - (nz - 1), 1),
            pltpu.roll(value, 1, 1),
        )

    copies[0].wait()
    copies[1].wait()
    kinds = 2 * count
    operators = disp_ref.shape[1]
    row = lax.broadcasted_iota(jnp.int32, (kinds, operators), 0)
    at = lax.broadcasted_iota(jnp.int32, (kinds, operators), 1).astype(jnp.float32)
    value = jnp.zeros((kinds, operators), jnp.int32)
    for slot, wanted in enumerate(VALUES):
        value = jnp.where(row // 2 == slot, wanted, value)
    hit = jnp.broadcast_to(disp_ref[...], (kinds, operators)) == value
    first = jnp.min(jnp.where(hit, at, operators), axis=1, keepdims=True)
    last = jnp.max(jnp.where(hit, at, -1.0), axis=1, keepdims=True)
    chosen = at == jnp.where(side == 0, first, last)
    momenta = mom_ref[...].astype(jnp.float32)
    steps = []
    for k, scale in enumerate((nz // nx, nz // ny, 1)):
        spread_out = jnp.broadcast_to(momenta[k : k + 1], (kinds, operators))
        total = jnp.sum(jnp.where(chosen, spread_out, 0.0), axis=1, keepdims=True)
        steps.append(total.astype(jnp.int32) * scale)
    lane = lax.broadcasted_iota(jnp.int32, (kinds, lanes), 1)
    kind = lax.broadcasted_iota(jnp.int32, (kinds, lanes), 0)
    x_true = (lane // nz + half_x * side) % nx
    plane = steps[0] * x_true + steps[2] * (lane % nz) - (kind % 2) * (nz // 4)
    waves = []
    for y in range(ny):
        turns = ((plane + steps[1] * y + nz // 2) & (nz - 1)) - nz // 2
        waves.append(jnp.cos(turns.astype(jnp.float32) * (2.0 * math.pi / nz)).T)

    copies[2].wait()
    copies[3].wait()
    pieces = [own_links_ref[:, x] for x in range(half_x)]
    pieces += [other_links_ref[:, x] for x in range(half_x)]
    links = jnp.concatenate(pieces, axis=-1)
    links_ref[...] = links
    for row in range(18):
        back_ref[row] = pltpu.roll(links[row], nz, 1)
        back_ref[18 + row] = z_behind(links[36 + row])

    copies[4].wait()
    copies[5].wait()

    def lay_out(y):
        field = []
        for c in range(6):
            blocks = [own_ref[c, x, y] for x in range(half_x)]
            blocks += [other_ref[c, x, y] for x in range(half_x)]
            field.append(jnp.concatenate(blocks, axis=0).astype(jnp.float32))
            vt_ref[c, y] = field[c].T
        for slot in range(count):
            cosine = jnp.broadcast_to(waves[y][:, 2 * slot : 2 * slot + 1], (lanes, eigen))
            sine = jnp.broadcast_to(waves[y][:, 2 * slot + 1 : 2 * slot + 2], (lanes, eigen))
            for a in range(3):
                real = field[a] * cosine - field[3 + a] * sine
                imag = field[a] * sine + field[3 + a] * cosine
                base = (y * 6 + 2 * a) * lanes
                left_ref[slot, pl.ds(base, lanes), :] = real.astype(jnp.bfloat16)
                left_ref[slot, pl.ds(base + lanes, lanes), :] = imag.astype(jnp.bfloat16)

    def fields(y):
        y_ahead = (y + 1) % ny
        y_behind = (y + ny - 1) % ny

        def chunk(e):
            rows = pl.ds(pl.multiple_of(e * ROWS, ROWS), ROWS)
            lower = pl.ds(pl.multiple_of(e * ROWS + eigen, ROWS), ROWS)

            def entries(ref, base, at):
                return lambda part, a, b: ref[base + part * 9 + a * 3 + b, pl.ds(at, 1), :]

            def put(value, moved):
                slot = VALUES.index(value)
                for a in range(3):
                    even = pl.ds((y * 6 + 2 * a) * lanes, lanes)
                    odd = pl.ds((y * 6 + 2 * a + 1) * lanes, lanes)
                    real = moved[a].astype(jnp.bfloat16)
                    imag = moved[3 + a].astype(jnp.bfloat16)
                    right_ref[slot, rows, even] = real
                    right_ref[slot, rows, odd] = imag
                    right_ref[slot, lower, even] = imag
                    right_ref[slot, lower, odd] = -real

            field = [vt_ref[c, y, rows, :] for c in range(6)]
            ahead = [pltpu.roll(f, lanes - nz, 1) for f in field]
            moved = link_product(entries(links_ref, 0, y), ahead, False)
            put(1, moved)
            total = moved
            ahead = [vt_ref[c, y_ahead, rows, :] for c in range(6)]
            moved = link_product(entries(links_ref, 18, y), ahead, False)
            put(2, moved)
            total = [p + q for p, q in zip(total, moved)]
            ahead = [z_ahead(f) for f in field]
            moved = link_product(entries(links_ref, 36, y), ahead, False)
            put(3, moved)
            total = [p + q for p, q in zip(total, moved)]
            behind = [pltpu.roll(f, nz, 1) for f in field]
            moved = link_product(entries(back_ref, 0, y), behind, True)
            total = [p + q for p, q in zip(total, moved)]
            behind = [vt_ref[c, y_behind, rows, :] for c in range(6)]
            moved = link_product(entries(links_ref, 18, y_behind), behind, True)
            total = [p + q for p, q in zip(total, moved)]
            behind = [z_behind(f) for f in field]
            moved = link_product(entries(back_ref, 18, y), behind, True)
            total = [p + q for p, q in zip(total, moved)]
            put(0, [f - t * (1.0 / 6.0) for f, t in zip(field, total)])

        lax.fori_loop(0, eigen // ROWS, lambda e, c: (chunk(e), c)[1], 0, unroll=UNROLL)

    for y in range(ny):
        lay_out(y)
    for y in range(ny):
        fields(y)
    for slot in range(count):
        total = jnp.dot(right_ref[slot], left_ref[slot], preferred_element_type=jnp.float32)
        total = (total * norm_factor).astype(jnp.bfloat16)
        phi_ref[slot] = jnp.concatenate([total[:eigen], total[eigen:]], axis=1)


def elementals(norm_factor, displacements, momenta, own, other, own_links, other_links):
    half_x, ny, nz, eigen = own.shape[1:]
    lanes = 2 * half_x * nz
    count = len(VALUES)
    vmem = pl.BlockSpec(memory_space=pltpu.VMEM)
    anywhere = pl.BlockSpec(memory_space=pltpu.HBM)
    operands = (displacements, momenta, own, other, own_links, other_links)
    return pl.pallas_call(
        functools.partial(elemental_kernel, norm_factor),
        out_shape=jax.ShapeDtypeStruct((count, eigen, 2 * eigen), jnp.bfloat16),
        in_specs=[anywhere] * 6,
        out_specs=vmem,
        scratch_shapes=[pltpu.VMEM(p.shape, p.dtype) for p in operands]
        + [
            pltpu.VMEM((6, ny, eigen, lanes), jnp.float32),
            pltpu.VMEM((54, ny, lanes), jnp.float32),
            pltpu.VMEM((36, ny, lanes), jnp.float32),
            pltpu.VMEM((count, 6 * ny * lanes, eigen), jnp.bfloat16),
            pltpu.VMEM((count, 2 * eigen, 6 * ny * lanes), jnp.bfloat16),
            pltpu.SemaphoreType.DMA((6,)),
        ],
        compiler_params=pltpu.CompilerParams(vmem_limit_bytes=65000 * 1024),
        cost_estimate=pl.CostEstimate(
            flops=count * 2 * 6 * ny * lanes * eigen * 2 * eigen,
            bytes_accessed=2 * own.size * 2,
            transcendentals=0,
        ),
        name="elementals",
    )(*operands)


def slice_behind(hops):
    count = lax.axis_size("tm")
    me = lax.axis_index("tm")
    place = jnp.where(me % 2 == 0, me // 2, count - (me + 1) // 2)
    at = (place - hops + count) % count
    return jnp.where(at < count // 2, 2 * at, 2 * (count - at) - 1)


def apart(sink, source):
    count = lax.axis_size("tm")
    return (sink - source + count) % count


def separation(index, ring):
    if not ring:
        return jnp.int32(index)
    hops = (index + 1) // 2 if index % 2 == 1 else -(index // 2)
    return apart(lax.axis_index("tm"), slice_behind(hops))


def add_to_table(table, product, slot, column):
    total = jnp.sum(jnp.sum(product, axis=0, keepdims=True), axis=1, keepdims=True)
    total = total * (1.0 / product.shape[0])
    row_at = lax.broadcasted_iota(jnp.int32, table.shape, 0)
    column_at = lax.broadcasted_iota(jnp.int32, table.shape, 1)
    return table + jnp.where((row_at == slot) & (column_at == column), total, 0.0)


def elemental_blocks(phi_ref):
    slots, eigen, _ = phi_ref.shape
    blocks = []
    for slot in range(slots):
        rows = phi_ref[slot]
        turned = jnp.concatenate([-rows[:, eigen:], rows[:, :eigen]], axis=1)
        blocks.append(jnp.concatenate([rows, turned], axis=0))
    return blocks


def sandwich_block(blocks, perams, mixed_ref):
    spins, eigen = len(perams), perams[0].shape[0]
    flipped, weights = [], []
    for peram in perams:
        real, imag = peram[:, :eigen], peram[:, eigen:]
        flipped.append(jnp.concatenate([real.T, imag.T], axis=1))
        weights.append(jnp.concatenate([real, -imag], axis=1))
        weights.append(jnp.concatenate([imag, real], axis=1))
    flipped = jnp.concatenate(flipped, axis=0)
    weights = jnp.concatenate(weights, axis=0)
    for slot, block in enumerate(blocks):
        mixed = jnp.dot(flipped, block, preferred_element_type=jnp.float32)
        mixed = mixed.astype(jnp.bfloat16)
        for a in range(spins):
            mixed_ref[
                slot * eigen : (slot + 1) * eigen, 2 * eigen * a : 2 * eigen * (a + 1)
            ] = mixed[a * eigen : (a + 1) * eigen]
    result = jnp.dot(
        mixed_ref[:, : 2 * eigen * spins], weights, preferred_element_type=jnp.float32
    )
    return result.reshape(len(blocks), eigen, 2 * eigen)


def far_kernel(behind_ref, ahead_ref, first_ref, second_ref, back_out, on_out, mixed_ref):
    count = lax.axis_size("tm")
    behind = slice_behind(count // 4)
    ahead = slice_behind(-(count // 4))
    for sink_ref, source_ref, peram_ref, out, column in (
        (behind_ref, ahead_ref, first_ref, back_out, apart(behind, ahead)),
        (ahead_ref, behind_ref, second_ref, on_out, apart(ahead, behind)),
    ):
        perams = [peram_ref[a] for a in range(peram_ref.shape[0])]
        result = sandwich_block(elemental_blocks(sink_ref), perams, mixed_ref)
        table = jnp.zeros(out.shape, jnp.float32)
        for slot in range(sink_ref.shape[0]):
            product = source_ref[slot].astype(jnp.float32) * result[slot]
            table = add_to_table(table, product, slot, column)
        out[...] = table


def far(behind, ahead, first, second, separations):
    slots, eigen, columns = behind.shape
    spins = first.shape[0]
    vmem = pl.BlockSpec(memory_space=pltpu.VMEM)
    table = jax.ShapeDtypeStruct((slots, separations), jnp.float32)
    return pl.pallas_call(
        far_kernel,
        out_shape=(table, table),
        in_specs=[vmem] * 4,
        out_specs=(vmem, vmem),
        scratch_shapes=[pltpu.VMEM((slots * eigen, spins * columns), jnp.bfloat16)],
        compiler_params=pltpu.CompilerParams(vmem_limit_bytes=16 * 1024 * 1024),
        cost_estimate=pl.CostEstimate(
            flops=8 * spins * slots * eigen * columns * columns,
            bytes_accessed=4 * behind.size,
            transcendentals=0,
        ),
        name="far",
    )(behind, ahead, first, second)


def sandwich_kernel(made, met, ring, extra, *refs):
    refs = list(refs)
    table_ref = refs.pop(0)
    extra_refs = [refs.pop(0) for _ in range(extra)]
    if made:
        phi_ref, peram_hbm = refs.pop(0), refs.pop(0)
    if met:
        before_ref = refs.pop(0)
        arrival_refs = [refs.pop(0) for _ in range(len(met))]
    table_out = refs.pop(0)
    if made:
        out_ref, peram_ref, mixed_ref, sems = refs
        copies = []
        for k, index in enumerate(made):
            copy = pltpu.make_async_copy(
                peram_hbm.at[separation(index, ring)], peram_ref.at[k], sems.at[k]
            )
            copy.start()
            copies.append(copy)
    table = table_ref[...]
    for extra_ref in extra_refs:
        table = table + extra_ref[...]
    if met:
        slots, eigen = before_ref.shape[1:3]
        for k, index in enumerate(met):
            column = separation(index, ring)
            for slot in range(slots):
                rows = arrival_refs[k][slot]
                product = rows.astype(jnp.float32) * before_ref[k, slot]
                table = add_to_table(table, product, slot, column)
    if made:
        slots, eigen, _ = phi_ref.shape
        blocks = elemental_blocks(phi_ref)
        for k, index in enumerate(made):
            copies[k].wait()
            perams = [peram_ref[k, a] for a in range(peram_ref.shape[1])]
            result = sandwich_block(blocks, perams, mixed_ref)
            if index == 0:
                for slot in range(slots):
                    product = phi_ref[slot].astype(jnp.float32) * result[slot]
                    table = add_to_table(table, product, slot, 0)
            else:
                out_ref[k - (made[0] == 0)] = result
    table_out[...] = table


def sandwich_step(table, phi, perambulators, made, before, arrivals, met, ring, extra=()):
    slots, eigen, columns = phi.shape
    separations, spins = perambulators.shape[:2]
    vmem = pl.BlockSpec(memory_space=pltpu.VMEM)
    operands, specs = [table, *extra], [vmem] * (1 + len(extra))
    shapes, scratch = [jax.ShapeDtypeStruct(table.shape, table.dtype)], []
    if made:
        operands += [phi, perambulators]
        specs += [vmem, pl.BlockSpec(memory_space=pltpu.HBM)]
        kept = len([k for k in made if k > 0])
        shapes.append(jax.ShapeDtypeStruct((kept, slots, eigen, columns), jnp.float32))
        scratch = [
            pltpu.VMEM((len(made),) + perambulators.shape[1:], perambulators.dtype),
            pltpu.VMEM((slots * eigen, spins * columns), jnp.bfloat16),
            pltpu.SemaphoreType.DMA((len(made),)),
        ]
    if met:
        operands += [before] + list(arrivals)
        specs += [vmem] * (1 + len(arrivals))
    work = 4 * spins * slots * eigen * columns * columns
    return pl.pallas_call(
        functools.partial(sandwich_kernel, tuple(made), tuple(met), ring, len(extra)),
        out_shape=tuple(shapes),
        in_specs=specs,
        out_specs=(vmem,) * len(shapes),
        scratch_shapes=scratch,
        compiler_params=pltpu.CompilerParams(vmem_limit_bytes=16 * 1024 * 1024),
        cost_estimate=pl.CostEstimate(
            flops=len(made) * work + 1000,
            bytes_accessed=len(made) * 2 * spins * eigen * columns + 1000,
            transcendentals=0,
        ),
        name="sandwich" + "".join(str(k) for k in made) + "_meet" + "".join(str(k) for k in met),
    )(*operands)


def turn_kernel(disp_ref, phi_ref, kept_ref, given_ref, place_out, own_out, other_out, whole_ref):
    slots, eigen, _ = phi_ref.shape
    half = eigen // 2
    side = lax.axis_index("space")
    for slot in range(slots):
        rows = phi_ref[slot]
        whole_ref[slot] = jnp.concatenate([rows[:, :eigen].T, rows[:, eigen:].T], axis=1)
    mine = pl.ds(pl.multiple_of(side * half, half), half)
    others = pl.ds(pl.multiple_of((1 - side) * half, half), half)
    kept_ref[...] = whole_ref[:, mine, :]
    given_ref[...] = whole_ref[:, others, :]
    column = lax.broadcasted_iota(jnp.int32, own_out.shape, 1)
    row = lax.broadcasted_iota(jnp.int32, own_out.shape, 0)
    for k, (out, last) in enumerate(((own_out, side), (other_out, 1 - side))):
        table = jnp.zeros(out.shape, jnp.float32)
        for slot, value in enumerate(VALUES):
            o = pick_operator(disp_ref, value, last)
            place_out[k * slots + slot] = o
            table = table + jnp.where((row == slot) & (column == o), 1.0, 0.0)
        out[...] = table


def turn(displacements, phi):
    slots, eigen, columns = phi.shape
    vmem = pl.BlockSpec(memory_space=pltpu.VMEM)
    smem = pl.BlockSpec(memory_space=pltpu.SMEM)
    half = jax.ShapeDtypeStruct((slots, eigen // 2, columns), phi.dtype)
    table = jax.ShapeDtypeStruct((slots, displacements.shape[0]), jnp.float32)
    return pl.pallas_call(
        turn_kernel,
        out_shape=(half, half, jax.ShapeDtypeStruct((2 * slots,), jnp.int32), table, table),
        in_specs=[smem, vmem],
        out_specs=(vmem, vmem, smem, vmem, vmem),
        scratch_shapes=[pltpu.VMEM(phi.shape, phi.dtype)],
        compiler_params=pltpu.CompilerParams(vmem_limit_bytes=4 * 1024 * 1024),
        cost_estimate=pl.CostEstimate(flops=1000, bytes_accessed=4 * phi.size, transcendentals=0),
        name="turn",
    )(displacements, phi)


def opposite_kernel(peram_hbm, first_ref, second_ref, sems):
    count = lax.axis_size("tm")
    opposite = apart(lax.axis_index("tm"), slice_behind(count // 2))
    spins = first_ref.shape[0]
    copies = []
    for k, out in enumerate((first_ref, second_ref)):
        rows = peram_hbm.at[opposite, pl.ds(k * spins, spins)]
        copies.append(pltpu.make_async_copy(rows, out, sems.at[k]))
        copies[-1].start()
    for copy in copies:
        copy.wait()


def opposite_perambulators(perambulators):
    vmem = pl.BlockSpec(memory_space=pltpu.VMEM)
    half = (perambulators.shape[1] // 2,) + perambulators.shape[2:]
    half = jax.ShapeDtypeStruct(half, perambulators.dtype)
    return pl.pallas_call(
        opposite_kernel,
        out_shape=(half, half),
        in_specs=[pl.BlockSpec(memory_space=pl.ANY)],
        out_specs=(vmem, vmem),
        scratch_shapes=[pltpu.SemaphoreType.DMA((2,))],
        compiler_params=pltpu.CompilerParams(vmem_limit_bytes=65000 * 1024),
        cost_estimate=pl.CostEstimate(flops=1000, bytes_accessed=1000000, transcendentals=0),
        name="opposite_perambulators",
    )(perambulators)


def order_kernel(place_ref, kept_ref, taken_ref, out_ref, sems):
    slots = kept_ref.shape[0]
    copies = []
    for k in range(2 * slots):
        rows = kept_ref.at[k] if k < slots else taken_ref.at[k - slots]
        copies.append(pltpu.make_async_copy(rows, out_ref.at[place_ref[k]], sems.at[k]))
    for copy in copies:
        copy.start()
    for copy in copies:
        copy.wait()


def order(places, kept, taken):
    vmem = pl.BlockSpec(memory_space=pltpu.VMEM)
    shape = (2 * kept.shape[0],) + kept.shape[1:]
    return pl.pallas_call(
        order_kernel,
        out_shape=jax.ShapeDtypeStruct(shape, kept.dtype),
        in_specs=[pl.BlockSpec(memory_space=pltpu.SMEM), vmem, vmem],
        out_specs=pl.BlockSpec(memory_space=pl.ANY),
        scratch_shapes=[pltpu.SemaphoreType.DMA((2 * kept.shape[0],))],
        compiler_params=pltpu.CompilerParams(vmem_limit_bytes=4 * 1024 * 1024),
        cost_estimate=pl.CostEstimate(flops=1000, bytes_accessed=8 * kept.size, transcendentals=0),
        name="order",
    )(places, kept, taken)


def ring_pairs(count, hops=1):
    around = list(range(0, count, 2)) + list(range(count - 1 - count % 2, 0, -2))
    ahead = [(around[k], around[(k + hops) % count]) for k in range(count)]
    return ahead, [(b, a) for a, b in ahead]


def body(vectors, gauge_links, perambulators, momenta, displacements):
    swap = [(0, 1), (1, 0)]
    half_x, ny, nz, eigen = vectors.shape[3:]
    own = vectors.reshape((6, half_x, ny, nz, eigen))
    own_links = gauge_links.reshape((54, half_x, ny, nz))
    other = lax.ppermute(own, "space", swap)
    other_links = lax.ppermute(own_links, "space", swap)
    norm_factor = 1.0 / math.sqrt(6.0 * 2 * half_x * ny * nz)
    operators = momenta.shape[0]
    slots = len(VALUES)
    count = lax.axis_size("tm")
    peram = perambulators[0]
    separations = peram.shape[0]
    ring = count == separations and count % 4 == 0
    ahead, behind = ring_pairs(count)
    if ring:
        two_ahead, two_behind = ring_pairs(count, count // 4)
        first, second = opposite_perambulators(peram)
        first = lax.ppermute(first, "tm", two_ahead)
        second = lax.ppermute(second, "tm", two_behind)
    phi = elementals(
        norm_factor, displacements.reshape((1, operators)), momenta.T, own, other, own_links, other_links
    )

    if ring:
        phi, first, second = lax.optimization_barrier((phi, first, second))

    table = jnp.zeros((slots, separations), jnp.float32)
    one_way = other_way = phi
    before, met, came, extra = None, [], [], ()
    steps = count // 2 if ring else separations // 2 + 1
    for step in range(1, steps):
        made = [2 * step - 1, 2 * step]
        made = [k for k in made if k < separations]
        if ring:
            if step == count // 4 + 1:
                middle = (one_way, other_way)
            one_way = lax.ppermute(one_way, "tm", ahead)
            other_way = lax.ppermute(other_way, "tm", behind)
            arrivals = [one_way, other_way]
        else:
            arrivals = []
            for _ in made:
                one_way = lax.ppermute(one_way, "tm", [(i, (i + 1) % count) for i in range(count)])
                arrivals.append(one_way)
        worked = [0] + made if step == 1 else made
        if ring and step == count // 4 + 1:
            back, on = far(*middle, first, second, separations)
            table, back, on = lax.optimization_barrier((table, back, on))
            extra = (lax.ppermute(back, "tm", two_behind), lax.ppermute(on, "tm", two_ahead))
        table, sands = sandwich_step(table, phi, peram, worked, before, came, met, ring)
        before, met, came = sands, made, arrivals
        if step == 2:
            kept, given, places, own_place, other_place = turn(displacements, phi)
            table, kept, given = lax.optimization_barrier((table, kept, given))
            taken = lax.ppermute(given, "space", swap)
        if step < steps - 1:
            one_way, other_way, table, phi = lax.optimization_barrier((one_way, other_way, table, phi))
            came = [one_way, other_way] if ring else arrivals
    (table,) = sandwich_step(table, phi, peram, [], before, came, met, ring, extra)
    other_table = lax.ppermute(table, "space", swap)

    rows = order(places, kept, taken)
    correlators = jnp.sum(
        own_place[:, :, None] * table[:, None] + other_place[:, :, None] * other_table[:, None], axis=0
    )
    return (rows[None], correlators[:, None, :])


def solution(mesh):
    return jax.shard_map(
        body,
        mesh=mesh,
        in_specs=(
            P(("cfg", "tm"), None, None, "space", None, None, None),
            P(("cfg", "tm"), None, None, None, None, "space", None, None),
            P(("cfg", "tm"), None, None, None, None),
            P(),
            P(),
        ),
        out_specs=(P(("cfg", "tm"), None, "space", None), P(None, ("cfg", "tm"), None)),
        check_vma=False,
    )
```

```python
import functools
import math

import jax
import jax.numpy as jnp
from jax import lax
from jax.experimental import pallas as pl
from jax.experimental.pallas import tpu as pltpu
from jax.sharding import PartitionSpec as P

VALUES = (2, 3, 1, 0)


def pick_operator(disp_ref, value, last):
    count = disp_ref.shape[0]
    first_seen = jnp.int32(count)
    last_seen = jnp.int32(-1)
    for o in range(count):
        hit = disp_ref[o] == value
        first_seen = jnp.where(hit, jnp.minimum(first_seen, o), first_seen)
        last_seen = jnp.where(hit, o, last_seen)
    return jnp.where(last == 0, first_seen, last_seen)


def elemental_kernel(
    norm_factor,
    disp_hbm,
    mom_hbm,
    own_hbm,
    other_hbm,
    own_links_hbm,
    other_links_hbm,
    phi_ref,
    disp_ref,
    mom_ref,
    field_ref,
    links_ref,
    rows_ref,
    total_ref,
    wave_ref,
    left_ref,
    right_ref,
    sems,
):
    _, nx, ny, nz, eigen = field_ref.shape
    half_x = nx // 2
    sites = nx * nz
    count = len(VALUES)
    block = 6 * nz
    side = lax.axis_index("space")
    first_half, second_half = pl.ds(0, half_x), pl.ds(half_x, half_x)
    pairs = (
        (disp_hbm, disp_ref),
        (mom_hbm, mom_ref),
        (own_links_hbm, links_ref.at[:, first_half]),
        (other_links_hbm, links_ref.at[:, second_half]),
        (own_hbm, field_ref.at[:, first_half]),
        (other_hbm, field_ref.at[:, second_half]),
    )
    copies = [pltpu.make_async_copy(s, d, sems.at[k]) for k, (s, d) in enumerate(pairs)]
    for copy in copies:
        copy.start()

    copies[0].wait()
    copies[1].wait()
    kinds = 2 * count
    operators = disp_ref.shape[1]
    row = lax.broadcasted_iota(jnp.int32, (kinds, operators), 0)
    at = lax.broadcasted_iota(jnp.int32, (kinds, operators), 1).astype(jnp.float32)
    value = jnp.zeros((kinds, operators), jnp.int32)
    for slot, wanted in enumerate(VALUES):
        value = jnp.where(row // 2 == slot, wanted, value)
    hit = jnp.broadcast_to(disp_ref[...], (kinds, operators)) == value
    first = jnp.min(jnp.where(hit, at, operators), axis=1, keepdims=True)
    last = jnp.max(jnp.where(hit, at, -1.0), axis=1, keepdims=True)
    chosen = at == jnp.where(side == 0, first, last)
    momenta = mom_ref[...].astype(jnp.float32)
    steps = []
    for k, scale in enumerate((nz // nx, nz // ny, 1)):
        spread_out = jnp.broadcast_to(momenta[k : k + 1], (kinds, operators))
        total = jnp.sum(jnp.where(chosen, spread_out, 0.0), axis=1, keepdims=True)
        steps.append(total.astype(jnp.int32) * scale)
    lane = lax.broadcasted_iota(jnp.int32, (kinds, sites), 1)
    kind = lax.broadcasted_iota(jnp.int32, (kinds, sites), 0)
    x_true = (lane // nz + half_x * side) % nx
    plane = steps[0] * x_true + steps[2] * (lane % nz) - (kind % 2) * (nz // 4)
    for y in range(ny):
        turns = ((plane + steps[1] * y + nz // 2) & (nz - 1)) - nz // 2
        wave_ref[y] = jnp.cos(turns.astype(jnp.float32) * (2.0 * math.pi / nz)).T

    copies[2].wait()
    copies[3].wait()
    wide = rows_ref.shape[-1]
    lane_at = lax.broadcasted_iota(jnp.int32, (nx, ny, wide), 2)
    lower = lane_at < block // 2
    first_z = lane_at % nz == 0
    nothing = jnp.zeros((nx, ny, wide - block), jnp.float32)
    for mu in range(3):
        for a in range(3):
            for way in range(2):
                pieces = []
                for part in range(2):
                    for b in range(3):
                        entry = a * 3 + b if way == 0 else b * 3 + a
                        pieces.append(links_ref[mu * 18 + part * 9 + entry])
                row = jnp.concatenate(pieces + [nothing], axis=-1)
                if way == 1:
                    row = jnp.where(lower, row, -row)
                elif mu == 2:
                    row = jnp.where(
                        first_z, pltpu.roll(row, wide - (nz - 1), 2), pltpu.roll(row, 1, 2)
                    )
                rows_ref[mu, way, a] = row

    z_row = lax.broadcasted_iota(jnp.int32, (nz, wide), 0)
    z_lane = lax.broadcasted_iota(jnp.int32, (nz, wide), 1)
    inside = z_lane < block
    z_lane = z_lane % nz
    masks = {
        0: inside & (z_lane == z_row),
        1: inside & (z_lane == (z_row + 1) % nz),
        -1: inside & (z_lane == (z_row + nz - 1) % nz),
    }
    no_rows = jnp.zeros((wide - block, 2 * eigen), jnp.bfloat16)
    half = block // 2

    def matrix(mu, way, x, y):
        mask = masks[0] if mu < 2 else masks[1 - 2 * way]
        parts = []
        for a in range(3):
            entries = rows_ref[mu, way, a, x, pl.ds(y, 1), :]
            parts.append(jnp.where(mask, entries, 0.0).astype(jnp.bfloat16))
        return parts

    for copy in copies[4:]:
        copy.wait()

    def plane_step(x, carry):
        x_ahead = (x + 1) % nx
        x_behind = (x + nx - 1) % nx
        for y in range(ny):
            y_ahead, y_behind = (y + 1) % ny, (y - 1) % ny
            base = (x * ny + y) * block
            parts = [field_ref[c, x, y] for c in range(6)]
            real, imag = jnp.concatenate(parts[:3], axis=0), jnp.concatenate(parts[3:], axis=0)
            source = jnp.concatenate(
                [
                    jnp.concatenate([real, imag], axis=1),
                    jnp.concatenate([-imag, real], axis=1),
                    no_rows,
                ],
                axis=0,
            )
            targets = ((0, 0, x_behind, y), (1, 0, x, y_behind), (2, 0, x, y))
            targets += ((0, 1, x_ahead, y), (1, 1, x, y_ahead), (2, 1, x, y))
            pieces = []
            for mu, way, tx, ty in targets:
                pieces += matrix(mu, way, x, y) if way == 1 else matrix(mu, way, tx, ty)
            given = jnp.dot(
                jnp.concatenate(pieces, axis=0), source, preferred_element_type=jnp.float32
            )
            for k, (mu, way, tx, ty) in enumerate(targets):
                moved = given[k * half : (k + 1) * half]
                if way == 0:
                    at = (tx * ny + ty) * block
                    reals = pl.ds(pl.multiple_of(at, half), half)
                    imags = pl.ds(pl.multiple_of(at + half, half), half)
                    right_ref[VALUES.index(mu + 1), reals, :] = moved[:, :eigen].astype(jnp.bfloat16)
                    right_ref[VALUES.index(mu + 1), imags, :] = moved[:, eigen:].astype(jnp.bfloat16)
                total_ref[k, tx, ty] = moved
            field = [p.astype(jnp.float32) for p in parts]
            waves = wave_ref[y, pl.ds(pl.multiple_of(x * nz, nz), nz), :]
            for slot in range(count):
                cosine = jnp.broadcast_to(waves[:, 2 * slot : 2 * slot + 1], (nz, eigen))
                sine = jnp.broadcast_to(waves[:, 2 * slot + 1 : 2 * slot + 2], (nz, eigen))
                for a in range(3):
                    real = (field[a] * cosine - field[3 + a] * sine).astype(jnp.bfloat16)
                    imag = (field[a] * sine + field[3 + a] * cosine).astype(jnp.bfloat16)
                    reals = pl.ds(pl.multiple_of(base + a * nz, nz), nz)
                    imags = pl.ds(pl.multiple_of(base + (3 + a) * nz, nz), nz)
                    left_ref[slot, reals, :eigen] = real
                    left_ref[slot, imags, :eigen] = imag
                    left_ref[slot, reals, eigen:] = -imag
                    left_ref[slot, imags, eigen:] = real
        return carry

    def smear_step(x, carry):
        for y in range(ny):
            base = (x * ny + y) * block
            total = total_ref[0, x, y]
            for k in range(1, 6):
                total = total + total_ref[k, x, y]
            total = total * (1.0 / 6.0)
            for part in range(2):
                field = jnp.concatenate([field_ref[3 * part + a, x, y] for a in range(3)], axis=0)
                smooth = field.astype(jnp.float32) - total[:, part * eigen : (part + 1) * eigen]
                at = pl.ds(pl.multiple_of(base + part * half, half), half)
                right_ref[VALUES.index(0), at, :] = smooth.astype(jnp.bfloat16)
        return carry

    lax.fori_loop(0, nx, plane_step, 0, unroll=4)
    lax.fori_loop(0, nx, smear_step, 0)
    for slot in range(count):
        total = lax.dot_general(
            right_ref[slot],
            left_ref[slot],
            (((0,), (0,)), ((), ())),
            preferred_element_type=jnp.float32,
        )
        phi_ref[slot] = (total * norm_factor).astype(jnp.bfloat16)


def elementals(norm_factor, displacements, momenta, own, other, own_links, other_links):
    half_x, ny, nz, eigen = own.shape[1:]
    nx = 2 * half_x
    count = len(VALUES)
    sites = 6 * nx * ny * nz
    vmem = pl.BlockSpec(memory_space=pltpu.VMEM)
    anywhere = pl.BlockSpec(memory_space=pltpu.HBM)
    return pl.pallas_call(
        functools.partial(elemental_kernel, norm_factor),
        out_shape=jax.ShapeDtypeStruct((count, eigen, 2 * eigen), jnp.bfloat16),
        in_specs=[anywhere] * 6,
        out_specs=vmem,
        scratch_shapes=[
            pltpu.VMEM(displacements.shape, displacements.dtype),
            pltpu.VMEM(momenta.shape, momenta.dtype),
            pltpu.VMEM((6, nx, ny, nz, eigen), own.dtype),
            pltpu.VMEM((54, nx, ny, nz), own_links.dtype),
            pltpu.VMEM((3, 2, 3, nx, ny, 8 * nz), jnp.float32),
            pltpu.VMEM((6, nx, ny, 3 * nz, 2 * eigen), jnp.float32),
            pltpu.VMEM((ny, nx * nz, 2 * count), jnp.float32),
            pltpu.VMEM((count, sites, 2 * eigen), jnp.bfloat16),
            pltpu.VMEM((count, sites, eigen), jnp.bfloat16),
            pltpu.SemaphoreType.DMA((6,)),
        ],
        compiler_params=pltpu.CompilerParams(vmem_limit_bytes=65000 * 1024),
        cost_estimate=pl.CostEstimate(
            flops=count * 2 * sites * eigen * 2 * eigen,
            bytes_accessed=2 * own.size * 2,
            transcendentals=0,
        ),
        name="elementals",
    )(displacements, momenta, own, other, own_links, other_links)


def slice_behind(hops):
    count = lax.axis_size("tm")
    me = lax.axis_index("tm")
    place = jnp.where(me % 2 == 0, me // 2, count - (me + 1) // 2)
    at = (place - hops + count) % count
    return jnp.where(at < count // 2, 2 * at, 2 * (count - at) - 1)


def apart(sink, source):
    count = lax.axis_size("tm")
    return (sink - source + count) % count


def separation(index, ring):
    if not ring:
        return jnp.int32(index)
    hops = (index + 1) // 2 if index % 2 == 1 else -(index // 2)
    return apart(lax.axis_index("tm"), slice_behind(hops))


def add_to_table(table, product, slot, column):
    total = jnp.sum(jnp.sum(product, axis=0, keepdims=True), axis=1, keepdims=True)
    total = total * (1.0 / product.shape[0])
    row_at = lax.broadcasted_iota(jnp.int32, table.shape, 0)
    column_at = lax.broadcasted_iota(jnp.int32, table.shape, 1)
    return table + jnp.where((row_at == slot) & (column_at == column), total, 0.0)


def elemental_blocks(phi_ref):
    slots, eigen, _ = phi_ref.shape
    blocks = []
    for slot in range(slots):
        rows = phi_ref[slot]
        turned = jnp.concatenate([-rows[:, eigen:], rows[:, :eigen]], axis=1)
        blocks.append(jnp.concatenate([rows, turned], axis=0))
    return blocks


def sandwich_block(blocks, perams, mixed_ref):
    spins, eigen = len(perams), perams[0].shape[0]
    flipped, weights = [], []
    for peram in perams:
        real, imag = peram[:, :eigen], peram[:, eigen:]
        flipped.append(jnp.concatenate([real.T, imag.T], axis=1))
        weights.append(jnp.concatenate([real, -imag], axis=1))
        weights.append(jnp.concatenate([imag, real], axis=1))
    flipped = jnp.concatenate(flipped, axis=0)
    weights = jnp.concatenate(weights, axis=0)
    for slot, block in enumerate(blocks):
        mixed = jnp.dot(flipped, block, preferred_element_type=jnp.float32)
        mixed = mixed.astype(jnp.bfloat16)
        for a in range(spins):
            mixed_ref[
                slot * eigen : (slot + 1) * eigen, 2 * eigen * a : 2 * eigen * (a + 1)
            ] = mixed[a * eigen : (a + 1) * eigen]
    result = jnp.dot(
        mixed_ref[:, : 2 * eigen * spins], weights, preferred_element_type=jnp.float32
    )
    return result.reshape(len(blocks), eigen, 2 * eigen)


def far_kernel(behind_ref, ahead_ref, first_ref, second_ref, back_out, on_out, mixed_ref):
    count = lax.axis_size("tm")
    behind = slice_behind(count // 4)
    ahead = slice_behind(-(count // 4))
    for sink_ref, source_ref, peram_ref, out, column in (
        (behind_ref, ahead_ref, first_ref, back_out, apart(behind, ahead)),
        (ahead_ref, behind_ref, second_ref, on_out, apart(ahead, behind)),
    ):
        perams = [peram_ref[a] for a in range(peram_ref.shape[0])]
        result = sandwich_block(elemental_blocks(sink_ref), perams, mixed_ref)
        table = jnp.zeros(out.shape, jnp.float32)
        for slot in range(sink_ref.shape[0]):
            product = source_ref[slot].astype(jnp.float32) * result[slot]
            table = add_to_table(table, product, slot, column)
        out[...] = table


def far(behind, ahead, first, second, separations):
    slots, eigen, columns = behind.shape
    spins = first.shape[0]
    vmem = pl.BlockSpec(memory_space=pltpu.VMEM)
    table = jax.ShapeDtypeStruct((slots, separations), jnp.float32)
    return pl.pallas_call(
        far_kernel,
        out_shape=(table, table),
        in_specs=[vmem] * 4,
        out_specs=(vmem, vmem),
        scratch_shapes=[pltpu.VMEM((slots * eigen, spins * columns), jnp.bfloat16)],
        compiler_params=pltpu.CompilerParams(vmem_limit_bytes=16 * 1024 * 1024),
        cost_estimate=pl.CostEstimate(
            flops=8 * spins * slots * eigen * columns * columns,
            bytes_accessed=4 * behind.size,
            transcendentals=0,
        ),
        name="far",
    )(behind, ahead, first, second)


def sandwich_kernel(made, met, ring, extra, *refs):
    refs = list(refs)
    table_ref = refs.pop(0)
    extra_refs = [refs.pop(0) for _ in range(extra)]
    if made:
        phi_ref, peram_hbm = refs.pop(0), refs.pop(0)
    if met:
        before_ref = refs.pop(0)
        arrival_refs = [refs.pop(0) for _ in range(len(met))]
    table_out = refs.pop(0)
    if made:
        out_ref, peram_ref, mixed_ref, sems = refs
        copies = []
        for k, index in enumerate(made):
            copy = pltpu.make_async_copy(
                peram_hbm.at[separation(index, ring)], peram_ref.at[k], sems.at[k]
            )
            copy.start()
            copies.append(copy)
    table = table_ref[...]
    for extra_ref in extra_refs:
        table = table + extra_ref[...]
    if met:
        slots, eigen = before_ref.shape[1:3]
        for k, index in enumerate(met):
            column = separation(index, ring)
            for slot in range(slots):
                rows = arrival_refs[k][slot]
                product = rows.astype(jnp.float32) * before_ref[k, slot]
                table = add_to_table(table, product, slot, column)
    if made:
        slots, eigen, _ = phi_ref.shape
        blocks = elemental_blocks(phi_ref)
        for k, index in enumerate(made):
            copies[k].wait()
            perams = [peram_ref[k, a] for a in range(peram_ref.shape[1])]
            result = sandwich_block(blocks, perams, mixed_ref)
            if index == 0:
                for slot in range(slots):
                    product = phi_ref[slot].astype(jnp.float32) * result[slot]
                    table = add_to_table(table, product, slot, 0)
            else:
                out_ref[k - (made[0] == 0)] = result
    table_out[...] = table


def sandwich_step(table, phi, perambulators, made, before, arrivals, met, ring, extra=()):
    slots, eigen, columns = phi.shape
    separations, spins = perambulators.shape[:2]
    vmem = pl.BlockSpec(memory_space=pltpu.VMEM)
    operands, specs = [table, *extra], [vmem] * (1 + len(extra))
    shapes, scratch = [jax.ShapeDtypeStruct(table.shape, table.dtype)], []
    if made:
        operands += [phi, perambulators]
        specs += [vmem, pl.BlockSpec(memory_space=pltpu.HBM)]
        kept = len([k for k in made if k > 0])
        shapes.append(jax.ShapeDtypeStruct((kept, slots, eigen, columns), jnp.float32))
        scratch = [
            pltpu.VMEM((len(made),) + perambulators.shape[1:], perambulators.dtype),
            pltpu.VMEM((slots * eigen, spins * columns), jnp.bfloat16),
            pltpu.SemaphoreType.DMA((len(made),)),
        ]
    if met:
        operands += [before] + list(arrivals)
        specs += [vmem] * (1 + len(arrivals))
    work = 4 * spins * slots * eigen * columns * columns
    return pl.pallas_call(
        functools.partial(sandwich_kernel, tuple(made), tuple(met), ring, len(extra)),
        out_shape=tuple(shapes),
        in_specs=specs,
        out_specs=(vmem,) * len(shapes),
        scratch_shapes=scratch,
        compiler_params=pltpu.CompilerParams(vmem_limit_bytes=16 * 1024 * 1024),
        cost_estimate=pl.CostEstimate(
            flops=len(made) * work + 1000,
            bytes_accessed=len(made) * 2 * spins * eigen * columns + 1000,
            transcendentals=0,
        ),
        name="sandwich" + "".join(str(k) for k in made) + "_meet" + "".join(str(k) for k in met),
    )(*operands)


def turn_kernel(disp_ref, phi_ref, kept_ref, given_ref, place_out, own_out, other_out, whole_ref):
    slots, eigen, _ = phi_ref.shape
    half = eigen // 2
    side = lax.axis_index("space")
    for slot in range(slots):
        rows = phi_ref[slot]
        whole_ref[slot] = jnp.concatenate([rows[:, :eigen].T, rows[:, eigen:].T], axis=1)
    mine = pl.ds(pl.multiple_of(side * half, half), half)
    others = pl.ds(pl.multiple_of((1 - side) * half, half), half)
    kept_ref[...] = whole_ref[:, mine, :]
    given_ref[...] = whole_ref[:, others, :]
    column = lax.broadcasted_iota(jnp.int32, own_out.shape, 1)
    row = lax.broadcasted_iota(jnp.int32, own_out.shape, 0)
    for k, (out, last) in enumerate(((own_out, side), (other_out, 1 - side))):
        table = jnp.zeros(out.shape, jnp.float32)
        for slot, value in enumerate(VALUES):
            o = pick_operator(disp_ref, value, last)
            place_out[k * slots + slot] = o
            table = table + jnp.where((row == slot) & (column == o), 1.0, 0.0)
        out[...] = table


def turn(displacements, phi):
    slots, eigen, columns = phi.shape
    vmem = pl.BlockSpec(memory_space=pltpu.VMEM)
    smem = pl.BlockSpec(memory_space=pltpu.SMEM)
    half = jax.ShapeDtypeStruct((slots, eigen // 2, columns), phi.dtype)
    table = jax.ShapeDtypeStruct((slots, displacements.shape[0]), jnp.float32)
    return pl.pallas_call(
        turn_kernel,
        out_shape=(half, half, jax.ShapeDtypeStruct((2 * slots,), jnp.int32), table, table),
        in_specs=[smem, vmem],
        out_specs=(vmem, vmem, smem, vmem, vmem),
        scratch_shapes=[pltpu.VMEM(phi.shape, phi.dtype)],
        compiler_params=pltpu.CompilerParams(vmem_limit_bytes=4 * 1024 * 1024),
        cost_estimate=pl.CostEstimate(flops=1000, bytes_accessed=4 * phi.size, transcendentals=0),
        name="turn",
    )(displacements, phi)


def opposite_kernel(peram_hbm, first_ref, second_ref, sems):
    count = lax.axis_size("tm")
    opposite = apart(lax.axis_index("tm"), slice_behind(count // 2))
    spins = first_ref.shape[0]
    copies = []
    for k, out in enumerate((first_ref, second_ref)):
        rows = peram_hbm.at[opposite, pl.ds(k * spins, spins)]
        copies.append(pltpu.make_async_copy(rows, out, sems.at[k]))
        copies[-1].start()
    for copy in copies:
        copy.wait()


def opposite_perambulators(perambulators):
    vmem = pl.BlockSpec(memory_space=pltpu.VMEM)
    half = (perambulators.shape[1] // 2,) + perambulators.shape[2:]
    half = jax.ShapeDtypeStruct(half, perambulators.dtype)
    return pl.pallas_call(
        opposite_kernel,
        out_shape=(half, half),
        in_specs=[pl.BlockSpec(memory_space=pl.ANY)],
        out_specs=(vmem, vmem),
        scratch_shapes=[pltpu.SemaphoreType.DMA((2,))],
        compiler_params=pltpu.CompilerParams(vmem_limit_bytes=65000 * 1024),
        cost_estimate=pl.CostEstimate(flops=1000, bytes_accessed=1000000, transcendentals=0),
        name="opposite_perambulators",
    )(perambulators)


def order_kernel(place_ref, kept_ref, taken_ref, out_ref, sems):
    slots = kept_ref.shape[0]
    copies = []
    for k in range(2 * slots):
        rows = kept_ref.at[k] if k < slots else taken_ref.at[k - slots]
        copies.append(pltpu.make_async_copy(rows, out_ref.at[place_ref[k]], sems.at[k]))
    for copy in copies:
        copy.start()
    for copy in copies:
        copy.wait()


def order(places, kept, taken):
    vmem = pl.BlockSpec(memory_space=pltpu.VMEM)
    shape = (2 * kept.shape[0],) + kept.shape[1:]
    return pl.pallas_call(
        order_kernel,
        out_shape=jax.ShapeDtypeStruct(shape, kept.dtype),
        in_specs=[pl.BlockSpec(memory_space=pltpu.SMEM), vmem, vmem],
        out_specs=pl.BlockSpec(memory_space=pl.ANY),
        scratch_shapes=[pltpu.SemaphoreType.DMA((2 * kept.shape[0],))],
        compiler_params=pltpu.CompilerParams(vmem_limit_bytes=4 * 1024 * 1024),
        cost_estimate=pl.CostEstimate(flops=1000, bytes_accessed=8 * kept.size, transcendentals=0),
        name="order",
    )(places, kept, taken)


def ring_pairs(count, hops=1):
    around = list(range(0, count, 2)) + list(range(count - 1 - count % 2, 0, -2))
    ahead = [(around[k], around[(k + hops) % count]) for k in range(count)]
    return ahead, [(b, a) for a, b in ahead]


def body(vectors, gauge_links, perambulators, momenta, displacements):
    swap = [(0, 1), (1, 0)]
    half_x, ny, nz, eigen = vectors.shape[3:]
    own = vectors.reshape((6, half_x, ny, nz, eigen))
    own_links = gauge_links.reshape((54, half_x, ny, nz))
    other = lax.ppermute(own, "space", swap)
    other_links = lax.ppermute(own_links, "space", swap)
    norm_factor = 1.0 / math.sqrt(6.0 * 2 * half_x * ny * nz)
    operators = momenta.shape[0]
    slots = len(VALUES)
    count = lax.axis_size("tm")
    peram = perambulators[0]
    separations = peram.shape[0]
    ring = count == separations and count % 4 == 0
    ahead, behind = ring_pairs(count)
    if ring:
        two_ahead, two_behind = ring_pairs(count, count // 4)
        first, second = opposite_perambulators(peram)
        first = lax.ppermute(first, "tm", two_ahead)
        second = lax.ppermute(second, "tm", two_behind)
    other, other_links = lax.optimization_barrier((other, other_links))
    phi = elementals(
        norm_factor, displacements.reshape((1, operators)), momenta.T, own, other, own_links, other_links
    )

    table = jnp.zeros((slots, separations), jnp.float32)
    one_way = other_way = phi
    if ring:
        phi, first, second = lax.optimization_barrier((phi, first, second))
    before, met, came, extra = None, [], [], ()
    steps = count // 2 if ring else separations // 2 + 1
    for step in range(1, steps):
        made = [2 * step - 1, 2 * step]
        made = [k for k in made if k < separations]
        if ring:
            if step == count // 4 + 1:
                middle = (one_way, other_way)
            one_way = lax.ppermute(one_way, "tm", ahead)
            other_way = lax.ppermute(other_way, "tm", behind)
            arrivals = [one_way, other_way]
        else:
            arrivals = []
            for _ in made:
                one_way = lax.ppermute(one_way, "tm", [(i, (i + 1) % count) for i in range(count)])
                arrivals.append(one_way)
        worked = [0] + made if step == 1 else made
        if ring and step == count // 4 + 1:
            back, on = far(*middle, first, second, separations)
            table, back, on = lax.optimization_barrier((table, back, on))
            extra = (lax.ppermute(back, "tm", two_behind), lax.ppermute(on, "tm", two_ahead))
        table, sands = sandwich_step(table, phi, peram, worked, before, came, met, ring)
        before, met, came = sands, made, arrivals
        if step == 2:
            kept, given, places, own_place, other_place = turn(displacements, phi)
            table, kept, given = lax.optimization_barrier((table, kept, given))
            taken = lax.ppermute(given, "space", swap)
        if step < steps - 1:
            one_way, other_way, table, phi = lax.optimization_barrier((one_way, other_way, table, phi))
            came = [one_way, other_way] if ring else arrivals
    (table,) = sandwich_step(table, phi, peram, [], before, came, met, ring, extra)
    other_table = lax.ppermute(table, "space", swap)

    rows = order(places, kept, taken)
    correlators = jnp.sum(
        own_place[:, :, None] * table[:, None] + other_place[:, :, None] * other_table[:, None], axis=0
    )
    return (rows[None], correlators[:, None, :])


def solution(mesh):
    return jax.shard_map(
        body,
        mesh=mesh,
        in_specs=(
            P(("cfg", "tm"), None, None, "space", None, None, None),
            P(("cfg", "tm"), None, None, None, None, "space", None, None),
            P(("cfg", "tm"), None, None, None, None),
            P(),
            P(),
        ),
        out_specs=(P(("cfg", "tm"), None, "space", None), P(None, ("cfg", "tm"), None)),
        check_vma=False,
    )
```

```python
import functools
import math

import jax
import jax.numpy as jnp
from jax import lax
from jax.experimental import pallas as pl
from jax.experimental.pallas import tpu as pltpu
from jax.sharding import PartitionSpec as P

VALUES = (2, 3, 1, 0)


def pick_operator(disp_ref, value, last):
    count = disp_ref.shape[0]
    first_seen = jnp.int32(count)
    last_seen = jnp.int32(-1)
    for o in range(count):
        hit = disp_ref[o] == value
        first_seen = jnp.where(hit, jnp.minimum(first_seen, o), first_seen)
        last_seen = jnp.where(hit, o, last_seen)
    return jnp.where(last == 0, first_seen, last_seen)


def elemental_kernel(
    norm_factor,
    disp_hbm,
    mom_hbm,
    own_hbm,
    other_hbm,
    own_links_hbm,
    other_links_hbm,
    phi_ref,
    disp_ref,
    mom_ref,
    field_ref,
    links_ref,
    rows_ref,
    total_ref,
    wave_ref,
    left_ref,
    right_ref,
    sems,
):
    _, nx, ny, nz, eigen = field_ref.shape
    half_x = nx // 2
    sites = nx * nz
    count = len(VALUES)
    block = 6 * nz
    side = lax.axis_index("space")
    first_half, second_half = pl.ds(0, half_x), pl.ds(half_x, half_x)
    pairs = (
        (disp_hbm, disp_ref),
        (mom_hbm, mom_ref),
        (own_links_hbm, links_ref.at[:, first_half]),
        (other_links_hbm, links_ref.at[:, second_half]),
        (own_hbm, field_ref.at[:, first_half]),
        (other_hbm, field_ref.at[:, second_half]),
    )
    copies = [pltpu.make_async_copy(s, d, sems.at[k]) for k, (s, d) in enumerate(pairs)]
    for copy in copies:
        copy.start()

    copies[0].wait()
    copies[1].wait()
    kinds = 2 * count
    operators = disp_ref.shape[1]
    row = lax.broadcasted_iota(jnp.int32, (kinds, operators), 0)
    at = lax.broadcasted_iota(jnp.int32, (kinds, operators), 1).astype(jnp.float32)
    value = jnp.zeros((kinds, operators), jnp.int32)
    for slot, wanted in enumerate(VALUES):
        value = jnp.where(row // 2 == slot, wanted, value)
    hit = jnp.broadcast_to(disp_ref[...], (kinds, operators)) == value
    first = jnp.min(jnp.where(hit, at, operators), axis=1, keepdims=True)
    last = jnp.max(jnp.where(hit, at, -1.0), axis=1, keepdims=True)
    chosen = at == jnp.where(side == 0, first, last)
    momenta = mom_ref[...].astype(jnp.float32)
    steps = []
    for k, scale in enumerate((nz // nx, nz // ny, 1)):
        spread_out = jnp.broadcast_to(momenta[k : k + 1], (kinds, operators))
        total = jnp.sum(jnp.where(chosen, spread_out, 0.0), axis=1, keepdims=True)
        steps.append(total.astype(jnp.int32) * scale)
    lane = lax.broadcasted_iota(jnp.int32, (kinds, sites), 1)
    kind = lax.broadcasted_iota(jnp.int32, (kinds, sites), 0)
    x_true = (lane // nz + half_x * side) % nx
    plane = steps[0] * x_true + steps[2] * (lane % nz) - (kind % 2) * (nz // 4)
    for y in range(ny):
        turns = ((plane + steps[1] * y + nz // 2) & (nz - 1)) - nz // 2
        wave_ref[y] = jnp.cos(turns.astype(jnp.float32) * (2.0 * math.pi / nz)).T

    copies[2].wait()
    copies[3].wait()
    wide = rows_ref.shape[-1]
    lane_at = lax.broadcasted_iota(jnp.int32, (nx, ny, wide), 2)
    lower = lane_at < block // 2
    first_z = lane_at % nz == 0
    nothing = jnp.zeros((nx, ny, wide - block), jnp.float32)
    for mu in range(3):
        for a in range(3):
            for way in range(2):
                pieces = []
                for part in range(2):
                    for b in range(3):
                        entry = a * 3 + b if way == 0 else b * 3 + a
                        pieces.append(links_ref[mu * 18 + part * 9 + entry])
                row = jnp.concatenate(pieces + [nothing], axis=-1)
                if way == 1:
                    row = jnp.where(lower, row, -row)
                elif mu == 2:
                    row = jnp.where(
                        first_z, pltpu.roll(row, wide - (nz - 1), 2), pltpu.roll(row, 1, 2)
                    )
                high = row.astype(jnp.bfloat16).astype(jnp.float32)
                rows_ref[0, mu, way, a] = high
                rows_ref[1, mu, way, a] = row - high

    z_row = lax.broadcasted_iota(jnp.int32, (nz, wide), 0)
    z_lane = lax.broadcasted_iota(jnp.int32, (nz, wide), 1)
    inside = z_lane < block
    z_lane = z_lane % nz
    masks = {
        0: inside & (z_lane == z_row),
        1: inside & (z_lane == (z_row + 1) % nz),
        -1: inside & (z_lane == (z_row + nz - 1) % nz),
    }
    no_rows = jnp.zeros((wide - block, 2 * eigen), jnp.bfloat16)
    half = block // 2

    def matrix(mu, way, x, y):
        mask = masks[0] if mu < 2 else masks[1 - 2 * way]
        parts = []
        for a in range(3):
            both = []
            for part in range(2):
                entries = rows_ref[part, mu, way, a, x, pl.ds(y, 1), :]
                both.append(jnp.where(mask, entries, 0.0).astype(jnp.bfloat16))
            parts.append(jnp.concatenate(both, axis=1))
        return parts

    for copy in copies[4:]:
        copy.wait()

    def plane_step(x, carry):
        x_ahead = (x + 1) % nx
        x_behind = (x + nx - 1) % nx
        for y in range(ny):
            y_ahead, y_behind = (y + 1) % ny, (y - 1) % ny
            base = (x * ny + y) * block
            parts = [field_ref[c, x, y] for c in range(6)]
            real, imag = jnp.concatenate(parts[:3], axis=0), jnp.concatenate(parts[3:], axis=0)
            source = jnp.concatenate(
                [
                    jnp.concatenate([real, imag], axis=1),
                    jnp.concatenate([-imag, real], axis=1),
                    no_rows,
                ],
                axis=0,
            )
            source = jnp.concatenate([source, source], axis=0)
            targets = ((0, 0, x_behind, y), (1, 0, x, y_behind), (2, 0, x, y))
            targets += ((0, 1, x_ahead, y), (1, 1, x, y_ahead), (2, 1, x, y))
            pieces = []
            for mu, way, tx, ty in targets:
                pieces += matrix(mu, way, x, y) if way == 1 else matrix(mu, way, tx, ty)
            given = jnp.dot(
                jnp.concatenate(pieces, axis=0), source, preferred_element_type=jnp.float32
            )
            for k, (mu, way, tx, ty) in enumerate(targets):
                moved = given[k * half : (k + 1) * half]
                if k == 2:
                    local = moved
                if way == 0:
                    at = (tx * ny + ty) * block
                    reals = pl.ds(pl.multiple_of(at, half), half)
                    imags = pl.ds(pl.multiple_of(at + half, half), half)
                    right_ref[VALUES.index(mu + 1), reals, :] = moved[:, :eigen].astype(jnp.bfloat16)
                    right_ref[VALUES.index(mu + 1), imags, :] = moved[:, eigen:].astype(jnp.bfloat16)
                if mu < 2:
                    total_ref[mu + 2 * way, tx, ty] = moved
            field = [p.astype(jnp.float32) for p in parts]
            here = jnp.concatenate(
                [jnp.concatenate(field[:3], axis=0), jnp.concatenate(field[3:], axis=0)], axis=1
            )
            total_ref[4, x, y] = here - (local + moved) * (1.0 / 6.0)
            waves = wave_ref[y, pl.ds(pl.multiple_of(x * nz, nz), nz), :]
            for slot in range(count):
                cosine = jnp.broadcast_to(waves[:, 2 * slot : 2 * slot + 1], (nz, eigen))
                sine = jnp.broadcast_to(waves[:, 2 * slot + 1 : 2 * slot + 2], (nz, eigen))
                for a in range(3):
                    real = (field[a] * cosine - field[3 + a] * sine).astype(jnp.bfloat16)
                    imag = (field[a] * sine + field[3 + a] * cosine).astype(jnp.bfloat16)
                    reals = pl.ds(pl.multiple_of(base + a * nz, nz), nz)
                    imags = pl.ds(pl.multiple_of(base + (3 + a) * nz, nz), nz)
                    left_ref[slot, reals, :eigen] = real
                    left_ref[slot, imags, :eigen] = imag
                    left_ref[slot, reals, eigen:] = -imag
                    left_ref[slot, imags, eigen:] = real
        return carry

    def project(slot):
        total = lax.dot_general(
            right_ref[slot],
            left_ref[slot],
            (((0,), (0,)), ((), ())),
            preferred_element_type=jnp.float32,
        )
        phi_ref[slot] = (total * norm_factor).astype(jnp.bfloat16)

    lax.fori_loop(0, nx, plane_step, 0, unroll=8)
    smeared = VALUES.index(0)
    for slot in range(count):
        if slot != smeared:
            project(slot)
    for x in range(nx):
        for y in range(ny):
            base = (x * ny + y) * block
            total = total_ref[0, x, y]
            for k in range(1, 4):
                total = total + total_ref[k, x, y]
            smooth = (total_ref[4, x, y] - total * (1.0 / 6.0)).astype(jnp.bfloat16)
            for part in range(2):
                rows = smooth[:, part * eigen : (part + 1) * eigen]
                right_ref[smeared, pl.ds(base + part * half, half), :] = rows
    project(smeared)


def elementals(norm_factor, displacements, momenta, own, other, own_links, other_links):
    half_x, ny, nz, eigen = own.shape[1:]
    nx = 2 * half_x
    count = len(VALUES)
    sites = 6 * nx * ny * nz
    vmem = pl.BlockSpec(memory_space=pltpu.VMEM)
    anywhere = pl.BlockSpec(memory_space=pltpu.HBM)
    return pl.pallas_call(
        functools.partial(elemental_kernel, norm_factor),
        out_shape=jax.ShapeDtypeStruct((count, eigen, 2 * eigen), jnp.bfloat16),
        in_specs=[anywhere] * 6,
        out_specs=vmem,
        scratch_shapes=[
            pltpu.VMEM(displacements.shape, displacements.dtype),
            pltpu.VMEM(momenta.shape, momenta.dtype),
            pltpu.VMEM((6, nx, ny, nz, eigen), own.dtype),
            pltpu.VMEM((54, nx, ny, nz), own_links.dtype),
            pltpu.VMEM((2, 3, 2, 3, nx, ny, 8 * nz), jnp.float32),
            pltpu.VMEM((5, nx, ny, 3 * nz, 2 * eigen), jnp.float32),
            pltpu.VMEM((ny, nx * nz, 2 * count), jnp.float32),
            pltpu.VMEM((count, sites, 2 * eigen), jnp.bfloat16),
            pltpu.VMEM((count, sites, eigen), jnp.bfloat16),
            pltpu.SemaphoreType.DMA((6,)),
        ],
        compiler_params=pltpu.CompilerParams(vmem_limit_bytes=65000 * 1024),
        cost_estimate=pl.CostEstimate(
            flops=count * 2 * sites * eigen * 2 * eigen,
            bytes_accessed=2 * own.size * 2,
            transcendentals=0,
        ),
        name="elementals",
    )(displacements, momenta, own, other, own_links, other_links)


def slice_behind(hops):
    count = lax.axis_size("tm")
    me = lax.axis_index("tm")
    place = jnp.where(me % 2 == 0, me // 2, count - (me + 1) // 2)
    at = (place - hops + count) % count
    return jnp.where(at < count // 2, 2 * at, 2 * (count - at) - 1)


def apart(sink, source):
    count = lax.axis_size("tm")
    return (sink - source + count) % count


def separation(index, ring):
    if not ring:
        return jnp.int32(index)
    hops = (index + 1) // 2 if index % 2 == 1 else -(index // 2)
    return apart(lax.axis_index("tm"), slice_behind(hops))


def add_to_table(table, product, slot, column):
    total = jnp.sum(jnp.sum(product, axis=0, keepdims=True), axis=1, keepdims=True)
    total = total * (1.0 / product.shape[0])
    row_at = lax.broadcasted_iota(jnp.int32, table.shape, 0)
    column_at = lax.broadcasted_iota(jnp.int32, table.shape, 1)
    return table + jnp.where((row_at == slot) & (column_at == column), total, 0.0)


def elemental_blocks(phi_ref):
    slots, eigen, _ = phi_ref.shape
    blocks = []
    for slot in range(slots):
        rows = phi_ref[slot]
        turned = jnp.concatenate([-rows[:, eigen:], rows[:, :eigen]], axis=1)
        blocks.append(jnp.concatenate([rows, turned], axis=0))
    return blocks


def sandwich_block(blocks, perams, mixed_ref):
    spins, eigen = len(perams), perams[0].shape[0]
    flipped, weights = [], []
    for peram in perams:
        real, imag = peram[:, :eigen], peram[:, eigen:]
        flipped.append(jnp.concatenate([real.T, imag.T], axis=1))
        weights.append(jnp.concatenate([real, -imag], axis=1))
        weights.append(jnp.concatenate([imag, real], axis=1))
    flipped = jnp.concatenate(flipped, axis=0)
    weights = jnp.concatenate(weights, axis=0)
    for slot, block in enumerate(blocks):
        mixed = jnp.dot(flipped, block, preferred_element_type=jnp.float32)
        mixed = mixed.astype(jnp.bfloat16)
        for a in range(spins):
            mixed_ref[
                slot * eigen : (slot + 1) * eigen, 2 * eigen * a : 2 * eigen * (a + 1)
            ] = mixed[a * eigen : (a + 1) * eigen]
    result = jnp.dot(
        mixed_ref[:, : 2 * eigen * spins], weights, preferred_element_type=jnp.float32
    )
    return result.reshape(len(blocks), eigen, 2 * eigen)


def far_kernel(behind_ref, ahead_ref, some_ref, rest_ref, back_out, mixed_ref):
    count = lax.axis_size("tm")
    hops = count // 4
    column = apart(slice_behind(hops), slice_behind(-hops))
    perams = [ref[a] for ref in (some_ref, rest_ref) for a in range(ref.shape[0])]
    result = sandwich_block(elemental_blocks(behind_ref), perams, mixed_ref)
    table = jnp.zeros(back_out.shape, jnp.float32)
    for slot in range(behind_ref.shape[0]):
        product = ahead_ref[slot].astype(jnp.float32) * result[slot]
        table = add_to_table(table, product, slot, column)
    back_out[...] = table


def far(behind, ahead, some, rest, separations):
    slots, eigen, columns = behind.shape
    spins = 2 * some.shape[0]
    vmem = pl.BlockSpec(memory_space=pltpu.VMEM)
    return pl.pallas_call(
        far_kernel,
        out_shape=jax.ShapeDtypeStruct((slots, separations), jnp.float32),
        in_specs=[vmem] * 4,
        out_specs=vmem,
        scratch_shapes=[pltpu.VMEM((slots * eigen, spins * columns), jnp.bfloat16)],
        compiler_params=pltpu.CompilerParams(vmem_limit_bytes=16 * 1024 * 1024),
        cost_estimate=pl.CostEstimate(
            flops=4 * spins * slots * eigen * columns * columns,
            bytes_accessed=4 * behind.size,
            transcendentals=0,
        ),
        name="far",
    )(behind, ahead, some, rest)


def sandwich_kernel(made, met, ring, extra, *refs):
    refs = list(refs)
    table_ref = refs.pop(0)
    extra_refs = [refs.pop(0) for _ in range(extra)]
    if made:
        phi_ref, peram_hbm = refs.pop(0), refs.pop(0)
    if met:
        before_ref = refs.pop(0)
        arrival_refs = [refs.pop(0) for _ in range(len(met))]
    table_out = refs.pop(0)
    if made:
        out_ref, peram_ref, mixed_ref, sems = refs
        copies = []
        for k, index in enumerate(made):
            copy = pltpu.make_async_copy(
                peram_hbm.at[separation(index, ring)], peram_ref.at[k], sems.at[k]
            )
            copy.start()
            copies.append(copy)
    table = table_ref[...]
    for extra_ref in extra_refs:
        table = table + extra_ref[...]
    if met:
        slots, eigen = before_ref.shape[1:3]
        for k, index in enumerate(met):
            column = separation(index, ring)
            for slot in range(slots):
                rows = arrival_refs[k][slot]
                product = rows.astype(jnp.float32) * before_ref[k, slot]
                table = add_to_table(table, product, slot, column)
    if made:
        slots, eigen, _ = phi_ref.shape
        blocks = elemental_blocks(phi_ref)
        for k, index in enumerate(made):
            copies[k].wait()
            perams = [peram_ref[k, a] for a in range(peram_ref.shape[1])]
            result = sandwich_block(blocks, perams, mixed_ref)
            if index == 0:
                for slot in range(slots):
                    product = phi_ref[slot].astype(jnp.float32) * result[slot]
                    table = add_to_table(table, product, slot, 0)
            else:
                out_ref[k - (made[0] == 0)] = result
    table_out[...] = table


def sandwich_step(table, phi, perambulators, made, before, arrivals, met, ring, extra=()):
    slots, eigen, columns = phi.shape
    separations, spins = perambulators.shape[:2]
    vmem = pl.BlockSpec(memory_space=pltpu.VMEM)
    operands, specs = [table, *extra], [vmem] * (1 + len(extra))
    shapes, scratch = [jax.ShapeDtypeStruct(table.shape, table.dtype)], []
    if made:
        operands += [phi, perambulators]
        specs += [vmem, pl.BlockSpec(memory_space=pltpu.HBM)]
        kept = len([k for k in made if k > 0])
        shapes.append(jax.ShapeDtypeStruct((kept, slots, eigen, columns), jnp.float32))
        scratch = [
            pltpu.VMEM((len(made),) + perambulators.shape[1:], perambulators.dtype),
            pltpu.VMEM((slots * eigen, spins * columns), jnp.bfloat16),
            pltpu.SemaphoreType.DMA((len(made),)),
        ]
    if met:
        operands += [before] + list(arrivals)
        specs += [vmem] * (1 + len(arrivals))
    work = 4 * spins * slots * eigen * columns * columns
    return pl.pallas_call(
        functools.partial(sandwich_kernel, tuple(made), tuple(met), ring, len(extra)),
        out_shape=tuple(shapes),
        in_specs=specs,
        out_specs=(vmem,) * len(shapes),
        scratch_shapes=scratch,
        compiler_params=pltpu.CompilerParams(vmem_limit_bytes=16 * 1024 * 1024),
        cost_estimate=pl.CostEstimate(
            flops=len(made) * work + 1000,
            bytes_accessed=len(made) * 2 * spins * eigen * columns + 1000,
            transcendentals=0,
        ),
        name="sandwich" + "".join(str(k) for k in made) + "_meet" + "".join(str(k) for k in met),
    )(*operands)


def turn_kernel(disp_ref, phi_ref, kept_ref, given_ref, place_out, own_out, other_out, whole_ref):
    slots, eigen, _ = phi_ref.shape
    half = eigen // 2
    side = lax.axis_index("space")
    for slot in range(slots):
        rows = phi_ref[slot]
        whole_ref[slot] = jnp.concatenate([rows[:, :eigen].T, rows[:, eigen:].T], axis=1)
    mine = pl.ds(pl.multiple_of(side * half, half), half)
    others = pl.ds(pl.multiple_of((1 - side) * half, half), half)
    kept_ref[...] = whole_ref[:, mine, :]
    given_ref[...] = whole_ref[:, others, :]
    column = lax.broadcasted_iota(jnp.int32, own_out.shape, 1)
    row = lax.broadcasted_iota(jnp.int32, own_out.shape, 0)
    for k, (out, last) in enumerate(((own_out, side), (other_out, 1 - side))):
        table = jnp.zeros(out.shape, jnp.float32)
        for slot, value in enumerate(VALUES):
            o = pick_operator(disp_ref, value, last)
            place_out[k * slots + slot] = o
            table = table + jnp.where((row == slot) & (column == o), 1.0, 0.0)
        out[...] = table


def turn(displacements, phi):
    slots, eigen, columns = phi.shape
    vmem = pl.BlockSpec(memory_space=pltpu.VMEM)
    smem = pl.BlockSpec(memory_space=pltpu.SMEM)
    half = jax.ShapeDtypeStruct((slots, eigen // 2, columns), phi.dtype)
    table = jax.ShapeDtypeStruct((slots, displacements.shape[0]), jnp.float32)
    return pl.pallas_call(
        turn_kernel,
        out_shape=(half, half, jax.ShapeDtypeStruct((2 * slots,), jnp.int32), table, table),
        in_specs=[smem, vmem],
        out_specs=(vmem, vmem, smem, vmem, vmem),
        scratch_shapes=[pltpu.VMEM(phi.shape, phi.dtype)],
        compiler_params=pltpu.CompilerParams(vmem_limit_bytes=4 * 1024 * 1024),
        cost_estimate=pl.CostEstimate(flops=1000, bytes_accessed=4 * phi.size, transcendentals=0),
        name="turn",
    )(displacements, phi)


def order_kernel(place_ref, kept_ref, taken_ref, out_ref, sems):
    slots = kept_ref.shape[0]
    copies = []
    for k in range(2 * slots):
        rows = kept_ref.at[k] if k < slots else taken_ref.at[k - slots]
        copies.append(pltpu.make_async_copy(rows, out_ref.at[place_ref[k]], sems.at[k]))
    for copy in copies:
        copy.start()
    for copy in copies:
        copy.wait()


def order(places, kept, taken):
    vmem = pl.BlockSpec(memory_space=pltpu.VMEM)
    shape = (2 * kept.shape[0],) + kept.shape[1:]
    return pl.pallas_call(
        order_kernel,
        out_shape=jax.ShapeDtypeStruct(shape, kept.dtype),
        in_specs=[pl.BlockSpec(memory_space=pltpu.SMEM), vmem, vmem],
        out_specs=pl.BlockSpec(memory_space=pl.ANY),
        scratch_shapes=[pltpu.SemaphoreType.DMA((2 * kept.shape[0],))],
        compiler_params=pltpu.CompilerParams(vmem_limit_bytes=4 * 1024 * 1024),
        cost_estimate=pl.CostEstimate(flops=1000, bytes_accessed=8 * kept.size, transcendentals=0),
        name="order",
    )(places, kept, taken)


def ring_pairs(count, hops=1):
    around = list(range(0, count, 2)) + list(range(count - 1 - count % 2, 0, -2))
    ahead = [(around[k], around[(k + hops) % count]) for k in range(count)]
    return ahead, [(b, a) for a, b in ahead]


def body(vectors, gauge_links, perambulators, momenta, displacements):
    swap = [(0, 1), (1, 0)]
    half_x, ny, nz, eigen = vectors.shape[3:]
    own = vectors.reshape((6, half_x, ny, nz, eigen))
    own_links = gauge_links.reshape((54, half_x, ny, nz))
    other = lax.ppermute(own, "space", swap)
    other_links = lax.ppermute(own_links, "space", swap)
    norm_factor = 1.0 / math.sqrt(6.0 * 2 * half_x * ny * nz)
    operators = momenta.shape[0]
    slots = len(VALUES)
    count = lax.axis_size("tm")
    peram = perambulators[0]
    separations = peram.shape[0]
    ring = count == separations and count % 4 == 0
    ahead, behind = ring_pairs(count)
    if ring:
        two_ahead, two_behind = ring_pairs(count, count // 4)
        opposite = apart(lax.axis_index("tm"), slice_behind(count // 2))
        spins = peram.shape[1] // 2
        start = (opposite, lax.axis_index("space") * spins, 0, 0)
        some = lax.dynamic_slice(peram, start, (1, spins) + peram.shape[2:])[0]
        some = lax.ppermute(some, "tm", two_ahead)
    other, other_links = lax.optimization_barrier((other, other_links))
    phi = elementals(
        norm_factor, displacements.reshape((1, operators)), momenta.T, own, other, own_links, other_links
    )

    table = jnp.zeros((slots, separations), jnp.float32)
    one_way = other_way = phi
    if ring:
        phi, some = lax.optimization_barrier((phi, some))
        rest = lax.ppermute(some, "space", swap)
    before, met, came, extra = None, [], [], ()
    steps = count // 2 if ring else separations // 2 + 1
    for step in range(1, steps):
        made = [2 * step - 1, 2 * step]
        made = [k for k in made if k < separations]
        if ring:
            if step == count // 4 + 1:
                middle = (one_way, other_way)
            one_way = lax.ppermute(one_way, "tm", ahead)
            other_way = lax.ppermute(other_way, "tm", behind)
            arrivals = [one_way, other_way]
        else:
            arrivals = []
            for _ in made:
                one_way = lax.ppermute(one_way, "tm", [(i, (i + 1) % count) for i in range(count)])
                arrivals.append(one_way)
        worked = [0] + made if step == 1 else made
        if ring and step == count // 4 + 1:
            back = far(*middle, some, rest, separations)
            table, back = lax.optimization_barrier((table, back))
            extra = (lax.ppermute(back, "tm", two_behind),)
        table, sands = sandwich_step(table, phi, peram, worked, before, came, met, ring)
        before, met, came = sands, made, arrivals
        if step == 2:
            kept, given, places, own_place, other_place = turn(displacements, phi)
            table, kept, given = lax.optimization_barrier((table, kept, given))
            taken = lax.ppermute(given, "space", swap)
        if step < steps - 1:
            one_way, other_way, table, phi = lax.optimization_barrier((one_way, other_way, table, phi))
            came = [one_way, other_way] if ring else arrivals
    (table,) = sandwich_step(table, phi, peram, [], before, came, met, ring, extra)
    other_table = lax.ppermute(table, "space", swap)

    rows = order(places, kept, taken)
    correlators = jnp.sum(
        own_place[:, :, None] * table[:, None] + other_place[:, :, None] * other_table[:, None], axis=0
    )
    return (rows[None], correlators[:, None, :])


def solution(mesh):
    return jax.shard_map(
        body,
        mesh=mesh,
        in_specs=(
            P(("cfg", "tm"), None, None, "space", None, None, None),
            P(("cfg", "tm"), None, None, None, None, "space", None, None),
            P(("cfg", "tm"), None, None, None, None),
            P(),
            P(),
        ),
        out_specs=(P(("cfg", "tm"), None, "space", None), P(None, ("cfg", "tm"), None)),
        check_vma=False,
    )
```

```python
import functools
import math

import jax
import jax.numpy as jnp
from jax import lax
from jax.experimental import pallas as pl
from jax.experimental.pallas import tpu as pltpu
from jax.sharding import PartitionSpec as P

VALUES = (2, 3, 1, 0)


def pick_operator(disp_ref, value, last):
    count = disp_ref.shape[0]
    first_seen = jnp.int32(count)
    last_seen = jnp.int32(-1)
    for o in range(count):
        hit = disp_ref[o] == value
        first_seen = jnp.where(hit, jnp.minimum(first_seen, o), first_seen)
        last_seen = jnp.where(hit, o, last_seen)
    return jnp.where(last == 0, first_seen, last_seen)


def elemental_kernel(
    norm_factor,
    disp_hbm,
    mom_hbm,
    own_hbm,
    other_hbm,
    own_links_hbm,
    other_links_hbm,
    phi_ref,
    disp_ref,
    mom_ref,
    field_ref,
    links_ref,
    rows_ref,
    total_ref,
    wave_ref,
    left_ref,
    right_ref,
    sems,
):
    _, nx, ny, nz, eigen = field_ref.shape
    half_x = nx // 2
    sites = nx * nz
    count = len(VALUES)
    block = 6 * nz
    side = lax.axis_index("space")
    first_half, second_half = pl.ds(0, half_x), pl.ds(half_x, half_x)
    pairs = (
        (disp_hbm, disp_ref),
        (mom_hbm, mom_ref),
        (own_links_hbm, links_ref.at[:, first_half]),
        (other_links_hbm, links_ref.at[:, second_half]),
        (own_hbm, field_ref.at[:, first_half]),
        (other_hbm, field_ref.at[:, second_half]),
    )
    copies = [pltpu.make_async_copy(s, d, sems.at[k]) for k, (s, d) in enumerate(pairs)]
    for copy in copies:
        copy.start()

    copies[0].wait()
    copies[1].wait()
    kinds = 2 * count
    operators = disp_ref.shape[1]
    row = lax.broadcasted_iota(jnp.int32, (kinds, operators), 0)
    at = lax.broadcasted_iota(jnp.int32, (kinds, operators), 1).astype(jnp.float32)
    value = jnp.zeros((kinds, operators), jnp.int32)
    for slot, wanted in enumerate(VALUES):
        value = jnp.where(row // 2 == slot, wanted, value)
    hit = jnp.broadcast_to(disp_ref[...], (kinds, operators)) == value
    first = jnp.min(jnp.where(hit, at, operators), axis=1, keepdims=True)
    last = jnp.max(jnp.where(hit, at, -1.0), axis=1, keepdims=True)
    chosen = at == jnp.where(side == 0, first, last)
    momenta = mom_ref[...].astype(jnp.float32)
    steps = []
    for k, scale in enumerate((nz // nx, nz // ny, 1)):
        spread_out = jnp.broadcast_to(momenta[k : k + 1], (kinds, operators))
        total = jnp.sum(jnp.where(chosen, spread_out, 0.0), axis=1, keepdims=True)
        steps.append(total.astype(jnp.int32) * scale)
    lane = lax.broadcasted_iota(jnp.int32, (kinds, sites), 1)
    kind = lax.broadcasted_iota(jnp.int32, (kinds, sites), 0)
    x_true = (lane // nz + half_x * side) % nx
    plane = steps[0] * x_true + steps[2] * (lane % nz) - (kind % 2) * (nz // 4)
    for y in range(ny):
        turns = ((plane + steps[1] * y + nz // 2) & (nz - 1)) - nz // 2
        wave_ref[y] = jnp.cos(turns.astype(jnp.float32) * (2.0 * math.pi / nz)).T

    copies[2].wait()
    copies[3].wait()
    wide = rows_ref.shape[-1]
    lane_at = lax.broadcasted_iota(jnp.int32, (nx, ny, wide), 2)
    lower = lane_at < block // 2
    first_z = lane_at % nz == 0
    nothing = jnp.zeros((nx, ny, wide - block), jnp.float32)
    for mu in range(3):
        for a in range(3):
            for way in range(2):
                pieces = []
                for part in range(2):
                    for b in range(3):
                        entry = a * 3 + b if way == 0 else b * 3 + a
                        pieces.append(links_ref[mu * 18 + part * 9 + entry])
                row = jnp.concatenate(pieces + [nothing], axis=-1)
                if way == 1:
                    row = jnp.where(lower, row, -row)
                elif mu == 2:
                    row = jnp.where(
                        first_z, pltpu.roll(row, wide - (nz - 1), 2), pltpu.roll(row, 1, 2)
                    )
                high = row.astype(jnp.bfloat16).astype(jnp.float32)
                rows_ref[0, mu, way, a] = high
                rows_ref[1, mu, way, a] = row - high

    z_row = lax.broadcasted_iota(jnp.int32, (nz, wide), 0)
    z_lane = lax.broadcasted_iota(jnp.int32, (nz, wide), 1)
    inside = z_lane < block
    z_lane = z_lane % nz
    masks = {
        0: inside & (z_lane == z_row),
        1: inside & (z_lane == (z_row + 1) % nz),
        -1: inside & (z_lane == (z_row + nz - 1) % nz),
    }
    no_rows = jnp.zeros((wide - block, 2 * eigen), jnp.bfloat16)
    half = block // 2

    def matrix(mu, way, x, y):
        mask = masks[0] if mu < 2 else masks[1 - 2 * way]
        parts = []
        for a in range(3):
            both = []
            for part in range(2):
                entries = rows_ref[part, mu, way, a, x, pl.ds(y, 1), :]
                both.append(jnp.where(mask, entries, 0.0).astype(jnp.bfloat16))
            parts.append(jnp.concatenate(both, axis=1))
        return parts

    for copy in copies[4:]:
        copy.wait()

    def plane_step(x, carry):
        x_ahead = (x + 1) % nx
        x_behind = (x + nx - 1) % nx
        for y in range(ny):
            y_ahead, y_behind = (y + 1) % ny, (y - 1) % ny
            base = (x * ny + y) * block
            parts = [field_ref[c, x, y] for c in range(6)]
            real, imag = jnp.concatenate(parts[:3], axis=0), jnp.concatenate(parts[3:], axis=0)
            source = jnp.concatenate(
                [
                    jnp.concatenate([real, imag], axis=1),
                    jnp.concatenate([-imag, real], axis=1),
                    no_rows,
                ],
                axis=0,
            )
            source = jnp.concatenate([source, source], axis=0)
            targets = ((0, 0, x_behind, y), (1, 0, x, y_behind), (2, 0, x, y))
            targets += ((0, 1, x_ahead, y), (1, 1, x, y_ahead), (2, 1, x, y))
            pieces = []
            for mu, way, tx, ty in targets:
                pieces += matrix(mu, way, x, y) if way == 1 else matrix(mu, way, tx, ty)
            given = jnp.dot(
                jnp.concatenate(pieces, axis=0), source, preferred_element_type=jnp.float32
            )
            for k, (mu, way, tx, ty) in enumerate(targets):
                moved = given[k * half : (k + 1) * half]
                if k == 2:
                    local = moved
                if way == 0:
                    at = (tx * ny + ty) * block
                    reals = pl.ds(pl.multiple_of(at, half), half)
                    imags = pl.ds(pl.multiple_of(at + half, half), half)
                    right_ref[VALUES.index(mu + 1), reals, :] = moved[:, :eigen].astype(jnp.bfloat16)
                    right_ref[VALUES.index(mu + 1), imags, :] = moved[:, eigen:].astype(jnp.bfloat16)
                if mu < 2:
                    total_ref[mu + 2 * way, tx, ty] = moved
            field = [p.astype(jnp.float32) for p in parts]
            here = jnp.concatenate(
                [jnp.concatenate(field[:3], axis=0), jnp.concatenate(field[3:], axis=0)], axis=1
            )
            total_ref[4, x, y] = here - (local + moved) * (1.0 / 6.0)
            waves = wave_ref[y, pl.ds(pl.multiple_of(x * nz, nz), nz), :]
            for slot in range(count):
                cosine = jnp.broadcast_to(waves[:, 2 * slot : 2 * slot + 1], (nz, eigen))
                sine = jnp.broadcast_to(waves[:, 2 * slot + 1 : 2 * slot + 2], (nz, eigen))
                for a in range(3):
                    real = (field[a] * cosine - field[3 + a] * sine).astype(jnp.bfloat16)
                    imag = (field[a] * sine + field[3 + a] * cosine).astype(jnp.bfloat16)
                    reals = pl.ds(pl.multiple_of(base + a * nz, nz), nz)
                    imags = pl.ds(pl.multiple_of(base + (3 + a) * nz, nz), nz)
                    left_ref[slot, reals, :eigen] = real
                    left_ref[slot, imags, :eigen] = imag
                    left_ref[slot, reals, eigen:] = -imag
                    left_ref[slot, imags, eigen:] = real
        return carry

    def project(slot):
        total = lax.dot_general(
            right_ref[slot],
            left_ref[slot],
            (((0,), (0,)), ((), ())),
            preferred_element_type=jnp.float32,
        )
        phi_ref[slot] = (total * norm_factor).astype(jnp.bfloat16)

    lax.fori_loop(0, nx, plane_step, 0, unroll=8)
    smeared = VALUES.index(0)
    for slot in range(count):
        if slot != smeared:
            project(slot)
    for x in range(nx):
        for y in range(ny):
            base = (x * ny + y) * block
            total = total_ref[0, x, y]
            for k in range(1, 4):
                total = total + total_ref[k, x, y]
            smooth = (total_ref[4, x, y] - total * (1.0 / 6.0)).astype(jnp.bfloat16)
            for part in range(2):
                rows = smooth[:, part * eigen : (part + 1) * eigen]
                right_ref[smeared, pl.ds(base + part * half, half), :] = rows
    project(smeared)


def elementals(norm_factor, displacements, momenta, own, other, own_links, other_links):
    half_x, ny, nz, eigen = own.shape[1:]
    nx = 2 * half_x
    count = len(VALUES)
    sites = 6 * nx * ny * nz
    vmem = pl.BlockSpec(memory_space=pltpu.VMEM)
    anywhere = pl.BlockSpec(memory_space=pltpu.HBM)
    return pl.pallas_call(
        functools.partial(elemental_kernel, norm_factor),
        out_shape=jax.ShapeDtypeStruct((count, eigen, 2 * eigen), jnp.bfloat16),
        in_specs=[anywhere] * 6,
        out_specs=vmem,
        scratch_shapes=[
            pltpu.VMEM(displacements.shape, displacements.dtype),
            pltpu.VMEM(momenta.shape, momenta.dtype),
            pltpu.VMEM((6, nx, ny, nz, eigen), own.dtype),
            pltpu.VMEM((54, nx, ny, nz), own_links.dtype),
            pltpu.VMEM((2, 3, 2, 3, nx, ny, 8 * nz), jnp.float32),
            pltpu.VMEM((5, nx, ny, 3 * nz, 2 * eigen), jnp.float32),
            pltpu.VMEM((ny, nx * nz, 2 * count), jnp.float32),
            pltpu.VMEM((count, sites, 2 * eigen), jnp.bfloat16),
            pltpu.VMEM((count, sites, eigen), jnp.bfloat16),
            pltpu.SemaphoreType.DMA((6,)),
        ],
        compiler_params=pltpu.CompilerParams(vmem_limit_bytes=65000 * 1024),
        cost_estimate=pl.CostEstimate(
            flops=16 * count * sites * eigen * 2 * eigen,
            bytes_accessed=2 * own.size * 2,
            transcendentals=0,
        ),
        name="elementals",
    )(displacements, momenta, own, other, own_links, other_links)


def slice_behind(hops):
    count = lax.axis_size("tm")
    me = lax.axis_index("tm")
    place = jnp.where(me % 2 == 0, me // 2, count - (me + 1) // 2)
    at = (place - hops + count) % count
    return jnp.where(at < count // 2, 2 * at, 2 * (count - at) - 1)


def apart(sink, source):
    count = lax.axis_size("tm")
    return (sink - source + count) % count


def separation(index, ring):
    if not ring:
        return jnp.int32(index)
    hops = (index + 1) // 2 if index % 2 == 1 else -(index // 2)
    return apart(lax.axis_index("tm"), slice_behind(hops))


def add_to_table(table, product, slot, column):
    total = jnp.sum(jnp.sum(product, axis=0, keepdims=True), axis=1, keepdims=True)
    total = total * (1.0 / product.shape[0])
    row_at = lax.broadcasted_iota(jnp.int32, table.shape, 0)
    column_at = lax.broadcasted_iota(jnp.int32, table.shape, 1)
    return table + jnp.where((row_at == slot) & (column_at == column), total, 0.0)


def elemental_blocks(phi_ref):
    slots, eigen, _ = phi_ref.shape
    blocks = []
    for slot in range(slots):
        rows = phi_ref[slot]
        turned = jnp.concatenate([-rows[:, eigen:], rows[:, :eigen]], axis=1)
        blocks.append(jnp.concatenate([rows, turned], axis=0))
    return blocks


def sandwich_block(blocks, perams, mixed_ref):
    spins, eigen = len(perams), perams[0].shape[0]
    flipped, weights = [], []
    for peram in perams:
        real, imag = peram[:, :eigen], peram[:, eigen:]
        flipped.append(jnp.concatenate([real.T, imag.T], axis=1))
        weights.append(jnp.concatenate([real, -imag], axis=1))
        weights.append(jnp.concatenate([imag, real], axis=1))
    flipped = jnp.concatenate(flipped, axis=0)
    weights = jnp.concatenate(weights, axis=0)
    for slot, block in enumerate(blocks):
        mixed = jnp.dot(flipped, block, preferred_element_type=jnp.float32)
        mixed = mixed.astype(jnp.bfloat16)
        for a in range(spins):
            mixed_ref[
                slot * eigen : (slot + 1) * eigen, 2 * eigen * a : 2 * eigen * (a + 1)
            ] = mixed[a * eigen : (a + 1) * eigen]
    result = jnp.dot(
        mixed_ref[:, : 2 * eigen * spins], weights, preferred_element_type=jnp.float32
    )
    return result.reshape(len(blocks), eigen, 2 * eigen)


def far_kernel(behind_ref, ahead_ref, some_ref, rest_ref, back_out, mixed_ref):
    count = lax.axis_size("tm")
    hops = count // 4
    column = apart(slice_behind(hops), slice_behind(-hops))
    perams = [ref[a] for ref in (some_ref, rest_ref) for a in range(ref.shape[0])]
    result = sandwich_block(elemental_blocks(behind_ref), perams, mixed_ref)
    table = jnp.zeros(back_out.shape, jnp.float32)
    for slot in range(behind_ref.shape[0]):
        product = ahead_ref[slot].astype(jnp.float32) * result[slot]
        table = add_to_table(table, product, slot, column)
    back_out[...] = table


def far(behind, ahead, some, rest, separations):
    slots, eigen, columns = behind.shape
    spins = 2 * some.shape[0]
    vmem = pl.BlockSpec(memory_space=pltpu.VMEM)
    return pl.pallas_call(
        far_kernel,
        out_shape=jax.ShapeDtypeStruct((slots, separations), jnp.float32),
        in_specs=[vmem] * 4,
        out_specs=vmem,
        scratch_shapes=[pltpu.VMEM((slots * eigen, spins * columns), jnp.bfloat16)],
        compiler_params=pltpu.CompilerParams(vmem_limit_bytes=16 * 1024 * 1024),
        cost_estimate=pl.CostEstimate(
            flops=4 * spins * slots * eigen * columns * columns,
            bytes_accessed=4 * behind.size,
            transcendentals=0,
        ),
        name="far",
    )(behind, ahead, some, rest)


def sandwich_kernel(made, met, ring, extra, *refs):
    refs = list(refs)
    table_ref = refs.pop(0)
    extra_refs = [refs.pop(0) for _ in range(extra)]
    if made:
        phi_ref, peram_hbm = refs.pop(0), refs.pop(0)
    if met:
        before_ref = refs.pop(0)
        arrival_refs = [refs.pop(0) for _ in range(len(met))]
    table_out = refs.pop(0)
    if made:
        out_ref, peram_ref, mixed_ref, sems = refs
        copies = []
        for k, index in enumerate(made):
            copy = pltpu.make_async_copy(
                peram_hbm.at[separation(index, ring)], peram_ref.at[k], sems.at[k]
            )
            copy.start()
            copies.append(copy)
    table = table_ref[...]
    for extra_ref in extra_refs:
        table = table + extra_ref[...]
    if met:
        slots, eigen = before_ref.shape[1:3]
        for k, index in enumerate(met):
            column = separation(index, ring)
            for slot in range(slots):
                rows = arrival_refs[k][slot]
                product = rows.astype(jnp.float32) * before_ref[k, slot]
                table = add_to_table(table, product, slot, column)
    if made:
        slots, eigen, _ = phi_ref.shape
        blocks = elemental_blocks(phi_ref)
        for k, index in enumerate(made):
            copies[k].wait()
            perams = [peram_ref[k, a] for a in range(peram_ref.shape[1])]
            result = sandwich_block(blocks, perams, mixed_ref)
            if index == 0:
                for slot in range(slots):
                    product = phi_ref[slot].astype(jnp.float32) * result[slot]
                    table = add_to_table(table, product, slot, 0)
            else:
                out_ref[k - (made[0] == 0)] = result
    table_out[...] = table


def sandwich_step(table, phi, perambulators, made, before, arrivals, met, ring, extra=()):
    slots, eigen, columns = phi.shape
    separations, spins = perambulators.shape[:2]
    vmem = pl.BlockSpec(memory_space=pltpu.VMEM)
    operands, specs = [table, *extra], [vmem] * (1 + len(extra))
    shapes, scratch = [jax.ShapeDtypeStruct(table.shape, table.dtype)], []
    if made:
        operands += [phi, perambulators]
        specs += [vmem, pl.BlockSpec(memory_space=pltpu.HBM)]
        kept = len([k for k in made if k > 0])
        shapes.append(jax.ShapeDtypeStruct((kept, slots, eigen, columns), jnp.float32))
        scratch = [
            pltpu.VMEM((len(made),) + perambulators.shape[1:], perambulators.dtype),
            pltpu.VMEM((slots * eigen, spins * columns), jnp.bfloat16),
            pltpu.SemaphoreType.DMA((len(made),)),
        ]
    if met:
        operands += [before] + list(arrivals)
        specs += [vmem] * (1 + len(arrivals))
    work = 4 * spins * slots * eigen * columns * columns
    return pl.pallas_call(
        functools.partial(sandwich_kernel, tuple(made), tuple(met), ring, len(extra)),
        out_shape=tuple(shapes),
        in_specs=specs,
        out_specs=(vmem,) * len(shapes),
        scratch_shapes=scratch,
        compiler_params=pltpu.CompilerParams(vmem_limit_bytes=16 * 1024 * 1024),
        cost_estimate=pl.CostEstimate(
            flops=len(made) * work + 1000,
            bytes_accessed=len(made) * 2 * spins * eigen * columns + 1000,
            transcendentals=0,
        ),
        name="sandwich" + "".join(str(k) for k in made) + "_meet" + "".join(str(k) for k in met),
    )(*operands)


def turn_kernel(disp_ref, phi_ref, kept_ref, given_ref, place_out, own_out, other_out, whole_ref):
    slots, eigen, _ = phi_ref.shape
    half = eigen // 2
    side = lax.axis_index("space")
    for slot in range(slots):
        rows = phi_ref[slot]
        whole_ref[slot] = jnp.concatenate([rows[:, :eigen].T, rows[:, eigen:].T], axis=1)
    mine = pl.ds(pl.multiple_of(side * half, half), half)
    others = pl.ds(pl.multiple_of((1 - side) * half, half), half)
    kept_ref[...] = whole_ref[:, mine, :]
    given_ref[...] = whole_ref[:, others, :]
    column = lax.broadcasted_iota(jnp.int32, own_out.shape, 1)
    row = lax.broadcasted_iota(jnp.int32, own_out.shape, 0)
    for k, (out, last) in enumerate(((own_out, side), (other_out, 1 - side))):
        table = jnp.zeros(out.shape, jnp.float32)
        for slot, value in enumerate(VALUES):
            o = pick_operator(disp_ref, value, last)
            place_out[k * slots + slot] = o
            table = table + jnp.where((row == slot) & (column == o), 1.0, 0.0)
        out[...] = table


def turn(displacements, phi):
    slots, eigen, columns = phi.shape
    vmem = pl.BlockSpec(memory_space=pltpu.VMEM)
    smem = pl.BlockSpec(memory_space=pltpu.SMEM)
    half = jax.ShapeDtypeStruct((slots, eigen // 2, columns), phi.dtype)
    table = jax.ShapeDtypeStruct((slots, displacements.shape[0]), jnp.float32)
    return pl.pallas_call(
        turn_kernel,
        out_shape=(half, half, jax.ShapeDtypeStruct((2 * slots,), jnp.int32), table, table),
        in_specs=[smem, vmem],
        out_specs=(vmem, vmem, smem, vmem, vmem),
        scratch_shapes=[pltpu.VMEM(phi.shape, phi.dtype)],
        compiler_params=pltpu.CompilerParams(vmem_limit_bytes=4 * 1024 * 1024),
        cost_estimate=pl.CostEstimate(flops=1000, bytes_accessed=4 * phi.size, transcendentals=0),
        name="turn",
    )(displacements, phi)


def order_kernel(place_ref, kept_ref, taken_ref, out_ref, sems):
    slots = kept_ref.shape[0]
    copies = []
    for k in range(2 * slots):
        rows = kept_ref.at[k] if k < slots else taken_ref.at[k - slots]
        copies.append(pltpu.make_async_copy(rows, out_ref.at[place_ref[k]], sems.at[k]))
    for copy in copies:
        copy.start()
    for copy in copies:
        copy.wait()


def order(places, kept, taken):
    vmem = pl.BlockSpec(memory_space=pltpu.VMEM)
    shape = (2 * kept.shape[0],) + kept.shape[1:]
    return pl.pallas_call(
        order_kernel,
        out_shape=jax.ShapeDtypeStruct(shape, kept.dtype),
        in_specs=[pl.BlockSpec(memory_space=pltpu.SMEM), vmem, vmem],
        out_specs=pl.BlockSpec(memory_space=pl.ANY),
        scratch_shapes=[pltpu.SemaphoreType.DMA((2 * kept.shape[0],))],
        compiler_params=pltpu.CompilerParams(vmem_limit_bytes=4 * 1024 * 1024),
        cost_estimate=pl.CostEstimate(flops=1000, bytes_accessed=8 * kept.size, transcendentals=0),
        name="order",
    )(places, kept, taken)


def ring_pairs(count, hops=1):
    around = list(range(0, count, 2)) + list(range(count - 1 - count % 2, 0, -2))
    ahead = [(around[k], around[(k + hops) % count]) for k in range(count)]
    return ahead, [(b, a) for a, b in ahead]


def body(vectors, gauge_links, perambulators, momenta, displacements):
    swap = [(0, 1), (1, 0)]
    half_x, ny, nz, eigen = vectors.shape[3:]
    own = vectors.reshape((6, half_x, ny, nz, eigen))
    own_links = gauge_links.reshape((54, half_x, ny, nz))
    other = lax.ppermute(own, "space", swap)
    other_links = lax.ppermute(own_links, "space", swap)
    norm_factor = 1.0 / math.sqrt(6.0 * 2 * half_x * ny * nz)
    operators = momenta.shape[0]
    slots = len(VALUES)
    count = lax.axis_size("tm")
    peram = perambulators[0]
    separations = peram.shape[0]
    ring = count == separations and count % 4 == 0
    ahead, behind = ring_pairs(count)
    if ring:
        two_ahead, two_behind = ring_pairs(count, count // 4)
        opposite = apart(lax.axis_index("tm"), slice_behind(count // 2))
        spins = peram.shape[1] // 2
        start = (opposite, lax.axis_index("space") * spins, 0, 0)
        some = lax.dynamic_slice(peram, start, (1, spins) + peram.shape[2:])[0]
        some = lax.ppermute(some, "tm", two_ahead)
    other, other_links = lax.optimization_barrier((other, other_links))
    phi = elementals(
        norm_factor, displacements.reshape((1, operators)), momenta.T, own, other, own_links, other_links
    )

    table = jnp.zeros((slots, separations), jnp.float32)
    one_way = other_way = phi
    if ring:
        phi, some = lax.optimization_barrier((phi, some))
        rest = lax.ppermute(some, "space", swap)
    before, met, came, extra = None, [], [], ()
    steps = count // 2 if ring else separations // 2 + 1
    for step in range(1, steps):
        made = [2 * step - 1, 2 * step]
        made = [k for k in made if k < separations]
        if ring:
            if step == count // 4 + 1:
                middle = (one_way, other_way)
            one_way = lax.ppermute(one_way, "tm", ahead)
            other_way = lax.ppermute(other_way, "tm", behind)
            arrivals = [one_way, other_way]
        else:
            arrivals = []
            for _ in made:
                one_way = lax.ppermute(one_way, "tm", [(i, (i + 1) % count) for i in range(count)])
                arrivals.append(one_way)
        worked = [0] + made if step == 1 else made
        if ring and step == count // 4 + 1:
            back = far(*middle, some, rest, separations)
            table, back = lax.optimization_barrier((table, back))
            extra = (lax.ppermute(back, "tm", two_behind),)
        table, sands = sandwich_step(table, phi, peram, worked, before, came, met, ring)
        before, met, came = sands, made, arrivals
        if step == 2:
            kept, given, places, own_place, other_place = turn(displacements, phi)
            table, kept, given = lax.optimization_barrier((table, kept, given))
            taken = lax.ppermute(given, "space", swap)
        if step < steps - 1:
            one_way, _ = lax.optimization_barrier((one_way, table))
            other_way, _ = lax.optimization_barrier((other_way, table))
            came = [one_way, other_way] if ring else arrivals
    (table,) = sandwich_step(table, phi, peram, [], before, came, met, ring, extra)
    other_table = lax.ppermute(table, "space", swap)

    rows = order(places, kept, taken)
    correlators = jnp.sum(
        own_place[:, :, None] * table[:, None] + other_place[:, :, None] * other_table[:, None], axis=0
    )
    return (rows[None], correlators[:, None, :])


def solution(mesh):
    return jax.shard_map(
        body,
        mesh=mesh,
        in_specs=(
            P(("cfg", "tm"), None, None, "space", None, None, None),
            P(("cfg", "tm"), None, None, None, None, "space", None, None),
            P(("cfg", "tm"), None, None, None, None),
            P(),
            P(),
        ),
        out_specs=(P(("cfg", "tm"), None, "space", None), P(None, ("cfg", "tm"), None)),
        check_vma=False,
    )
```
